128 devices in a mesh: ctx: 16 (over y, x), mem: 8 (over z, core).
Axes of the slice: x: 4, y: 4, z: 4, core: 2. Of those that a mesh axis runs over, the one named last changes fastest.
Arguments:
- tokens: bfloat16 [16384, 4096], P(('ctx', 'mem')), may hold values from -6 to 6
- picks: int32 [16384, 2], P(('ctx', 'mem')), may hold values from 0 to 15, all different within a row; in each aligned block of 128 rows (0 to 127, 128 to 255, ...) at most 24 rows name the same one
- route_weight: bfloat16 [16384, 2], P(('ctx', 'mem')), may hold values from 0.19921875 to 1
- cotangent: bfloat16 [16384, 256], P(('ctx', 'mem')), may hold values from -6 to 6
- query_weight: bfloat16 [4096, 256], replicated, may hold values from -0.09375 to 0.09375
- key_weight: bfloat16 [4096, 16, 256], P('ctx', 'mem'), may hold values from -0.09375 to 0.09375
- value_weight: bfloat16 [4096, 16, 256], P('ctx', 'mem'), may hold values from -0.09375 to 0.09375
- gates: float32 [16, 3, 16], P('ctx', None, 'mem'), may hold values from 0 to 1, as said below
Outputs:
- token_grad: bfloat16 [16384, 4096], P(('ctx', 'mem'))
- key_grad: float32 [4096, 16, 256], P('ctx', 'mem')
- value_grad: float32 [4096, 16, 256], P('ctx', 'mem')
The draws below stay inside these ranges and needn't reach their ends.
Inputs may be any that keep to these rules, and one draw needn't show every extreme that they name: `picks`: each row names two different memories; within the 128 rows of one device no memory is named by more than 24 rows. `gates`: every entry lies strictly between 0 and 1.
All inputs are finite; a program needn't handle non-finite values.
Results may differ from the reference program's by a relative error of at most 0.023.
Values may be sent and summed in bfloat16 or wider, within the bound.
A program may use at most 128 MiB of HBM per device.

```python
import math
import jax
import jax.numpy as jnp
import numpy as np
from jax import lax

D = 4096
DK = 256
TOK_DEV = 128
STORE_NUMBER = 16
SEGMENT_TOTAL = 16
TOKENS = 16384
CAP = 24
N_CTX = 16
N_MEM = 8


def draw_gates(key, part):
    key = jax.random.fold_in(key, 7)
    concurrent_streams = jax.random.split(key, 6)
    slow_share = 0.5
    slow_store_selector = (jax.random.uniform(concurrent_streams[0], (1, STORE_NUMBER)) < slow_share).astype(jnp.float32)
    slow_step_size = jax.random.uniform(concurrent_streams[1], (SEGMENT_TOTAL, STORE_NUMBER), minval=0.3, maxval=1.0) / SEGMENT_TOTAL
    fast_step_size = jax.random.uniform(concurrent_streams[2], (SEGMENT_TOTAL, STORE_NUMBER), minval=0.7, maxval=2.2)
    span_sizes_list = (jax.random.uniform(concurrent_streams[3], (SEGMENT_TOTAL, STORE_NUMBER)) < 2.0 / SEGMENT_TOTAL).astype(jnp.float32)
    decay_multiplier = jnp.exp(-(slow_store_selector * slow_step_size + (1.0 - slow_store_selector) * fast_step_size)) * (1.0 - 0.45 * span_sizes_list)
    momentum = jax.random.uniform(concurrent_streams[4], (SEGMENT_TOTAL, STORE_NUMBER), minval=0.2, maxval=0.8)
    write_rate = jnp.exp(jax.random.uniform(concurrent_streams[5], (SEGMENT_TOTAL, STORE_NUMBER), minval=-5.3, maxval=-3.9))
    return jnp.stack([momentum, decay_multiplier, write_rate], axis=1).astype(jnp.float32)


def shard_levels(stream_key, extent, cuts, smallest, high):
    def one(axis_at, blocks):
        draws = jax.random.uniform(jax.random.fold_in(jax.random.fold_in(stream_key, 6), axis_at), (blocks,), jnp.float32, smallest / len(cuts), high / len(cuts))
        return jnp.repeat(jnp.exp(draws), extent[axis_at] // blocks).reshape((-1,) + (1,) * (len(extent) - axis_at - 1))

    factor_of = one(*cuts[0])
    for cut in cuts[1:]:
        factor_of = factor_of * one(*cut)
    return factor_of


def deal_out(key, own, number, rows, amount, top, bound, lean):
    order = jax.random.permutation(key, amount)
    packed, common = shares(amount, rows * top, bound, lean, True), shares(amount, rows * top, bound, lean, False)
    places = jnp.arange(amount)

    def named(lengths, offset_by):
        used = int((lengths > 0).sum())
        fixed = max(1, used // 4)
        shifted = fixed + (places - fixed + offset_by * (used - fixed)) % max(1, amount - fixed)
        return jnp.zeros((amount,), jnp.int32).at[order[jnp.where(places < fixed, places, shifted)]].set(jnp.asarray(lengths, jnp.int32))

    lengths = jnp.where(number % 4 == 0, named(packed, number // 4), named(common, number - number // 4 - 1))
    mixed = jax.random.permutation(jax.random.fold_in(own, 3), amount)
    donor, receiver = mixed[0:amount // 2 * 2:2], mixed[1:amount // 2 * 2:2]
    margin = jnp.minimum(lengths[donor] - 1, bound - lengths[receiver]) // 2
    margin = jnp.where((donor == order[0]) | (receiver == order[0]) | (lengths[receiver] == 0), 0, jnp.maximum(margin, 0))
    shifted = jax.random.randint(jax.random.fold_in(own, 4), (amount // 2,), 0, 1 << 20) % (margin + 1)
    lengths = lengths.at[donor].add(-shifted).at[receiver].add(shifted)
    members = jnp.searchsorted(jnp.cumsum(lengths), jnp.arange(rows * top), side="right").astype(jnp.int32)
    listing = members.reshape(top, rows).T
    listing = listing[jax.random.permutation(jax.random.fold_in(own, 1), rows)]
    offset_by = jax.random.randint(jax.random.fold_in(own, 2), (rows, 1), 0, top)
    return jnp.take_along_axis(listing, (jnp.arange(top)[None, :] + offset_by) % top, axis=1)


def shares(amount, total, limit, slope, full):
    weights = [(1 << 20) // math.isqrt(standing ** slope) + 1 for standing in range(1, amount + 1)]
    largest = limit if full else min(limit, max(-(-total // amount), total * weights[0] // sum(weights)))
    least = 1 if total - largest >= amount - 1 else 0
    given, spare = [largest] + [least] * (amount - 1), total - largest - least * (amount - 1)
    while spare > 0:
        candidates = [i for i in range(1, amount) if given[i] < largest] or [i for i in range(1, amount) if given[i] < limit]
        whole, left = sum([weights[i] for i in candidates]), spare
        for i in candidates:
            extra = min(limit - given[i], max(1, left * weights[i] // whole), spare)
            given[i] = given[i] + extra
            spare = spare - extra
    return np.array(given)


def centred(own_key, dims, scale, reach, pieces=(), kind=jnp.bfloat16):
    array = scale * jax.random.normal(own_key, dims, jnp.float32)
    if pieces:
        array = array * shard_levels(own_key, dims, pieces, -0.22, 0.18)
    return jnp.clip(array, -reach, reach).astype(kind)


def setup_inputs(seed: int = 0) -> dict:
    streams_of = jax.random.split(jax.random.key(seed), 9)
    tokens = centred(streams_of[0], (TOKENS, D), 1.0, 6.0, ((0, 128),))
    picks_keys = jax.random.split(jax.random.fold_in(streams_of[1], 1), TOKENS // TOK_DEV)
    picks_turns = jax.random.permutation(jax.random.fold_in(streams_of[1], 3), TOKENS // TOK_DEV)
    picks = jax.vmap(lambda own, number: deal_out(jax.random.fold_in(streams_of[1], 2), own, number, TOK_DEV, STORE_NUMBER, 2, CAP, 2))(picks_keys, picks_turns).reshape((TOKENS, 2))
    route_weight = jnp.clip(0.19921875 + 0.80078125 * jax.random.uniform(streams_of[2], (TOKENS, 2), jnp.float32) ** shard_levels(streams_of[2], (TOKENS, 2), ((0, 128),), -0.2, 0.2), 0.19921875, 1.0).astype(jnp.bfloat16)
    cotangent = centred(streams_of[3], (TOKENS, DK), 1.0, 6.0, ((0, 128),))
    query_weight = centred(streams_of[4], (D, DK), D ** -0.5, 0.09375)
    key_weight = centred(streams_of[5], (D, STORE_NUMBER, DK), D ** -0.5, 0.09375, ((0, 16), (1, 8)))
    value_weight = centred(streams_of[6], (D, STORE_NUMBER, DK), D ** -0.5, 0.09375, ((0, 16), (1, 8)))
    gates = draw_gates(jax.random.fold_in(streams_of[8], 71), 0)
    return {"tokens": tokens, "picks": picks, "route_weight": route_weight, "cotangent": cotangent, "query_weight": query_weight, "key_weight": key_weight, "value_weight": value_weight, "gates": gates}


def reference(tokens, picks, route_weight, cotangent, query_weight, key_weight, value_weight, gates):
    half = jnp.bfloat16
    single = jnp.float32
    blocks = N_CTX * N_MEM
    slot_rows = N_MEM * CAP
    query_rows = jnp.dot(tokens, query_weight, preferred_element_type=single).astype(half)
    weighted = (route_weight.astype(single)[:, :, None] * cotangent.astype(single)[:, None, :]).astype(half)
    block_ids = picks.reshape(blocks, 2 * TOK_DEV)
    onehot = (block_ids[:, :, None] == jnp.arange(STORE_NUMBER, dtype=jnp.int32)[None, None, :]).astype(jnp.int32)
    slot_index = jnp.sum((jnp.cumsum(onehot, axis=1) - onehot) * onehot, axis=2)
    block_number = jnp.arange(blocks, dtype=jnp.int32)[:, None]
    group_number = block_number // N_MEM
    source_number = block_number % N_MEM
    flat_index = (((block_ids * N_CTX + group_number) * N_MEM + source_number) * CAP + slot_index).reshape(-1)
    pick_order = jnp.arange(2 * TOKENS, dtype=jnp.int32)
    total_slots = STORE_NUMBER * N_CTX * slot_rows
    token_table = jnp.full((total_slots,), TOKENS, jnp.int32).at[flat_index].set(pick_order // 2)
    pick_table = jnp.full((total_slots,), 2 * TOKENS, jnp.int32).at[flat_index].set(pick_order)
    token_table = token_table.reshape(STORE_NUMBER, N_CTX, slot_rows)
    pick_table = pick_table.reshape(STORE_NUMBER, N_CTX, slot_rows)
    padded_tokens = jnp.concatenate([tokens, jnp.zeros((1, D), half)], axis=0)
    pick_side = jnp.concatenate([jnp.broadcast_to(query_rows[:, None, :], weighted.shape), weighted], axis=2)
    pick_side = jnp.concatenate([pick_side.reshape(2 * TOKENS, 2 * DK), jnp.zeros((1, 2 * DK), half)], axis=0)

    def one_memory(grad_sum, inputs):
        table_tok, table_pick, key_proj, value_proj, gate_rows = inputs
        owned_rows = padded_tokens[table_tok]
        side_rows = pick_side[table_pick]
        owned_queries = side_rows[:, :, :DK]
        owned_weighted = side_rows[:, :, DK:]
        flat_rows = owned_rows.reshape(N_CTX * slot_rows, D)
        key_rows = jnp.dot(flat_rows, key_proj, preferred_element_type=single).astype(half).reshape(N_CTX, slot_rows, DK)
        value_rows = jnp.dot(flat_rows, value_proj, preferred_element_type=single).astype(half).reshape(N_CTX, slot_rows, DK)
        momentum = gate_rows[:, 0]
        decay_multiplier = gate_rows[:, 1]
        write_rate = gate_rows[:, 2]
        written = write_rate[:, None, None] * jnp.einsum('cra,crb->cab', value_rows.astype(single), key_rows.astype(single))
        direct = jnp.einsum('cra,crb->cab', owned_weighted.astype(single), owned_queries.astype(single))
        zero_block = jnp.zeros((DK, DK), single)

        def forward(carry, step):
            state_prev, memory_prev = carry
            write_now, moment_now, retain_now = step
            state_now = moment_now * state_prev + write_now
            memory_now = retain_now * memory_prev + state_now
            return (state_now, memory_now), memory_now

        unused, memory = lax.scan(forward, (zero_block, zero_block), (written, momentum, decay_multiplier))

        def backward(carry, step):
            carry_total, carry_adjoint = carry
            direct_now, moment_now, retain_now = step
            total_now = direct_now + carry_total
            adjoint_now = total_now + carry_adjoint
            return (retain_now * total_now, moment_now * adjoint_now), adjoint_now

        unused, adjoint = lax.scan(backward, (zero_block, zero_block), (direct, momentum, decay_multiplier), reverse=True)
        memory_half = memory.astype(half)
        scaled = (write_rate[:, None, None] * adjoint).astype(half)
        query_grad = jnp.einsum('cra,cab->crb', owned_weighted.astype(single), memory_half.astype(single)).astype(half)
        value_grad_rows = jnp.einsum('crb,cab->cra', key_rows.astype(single), scaled.astype(single)).astype(half)
        key_grad_rows = jnp.einsum('cra,cab->crb', value_rows.astype(single), scaled.astype(single)).astype(half)
        contribution = jnp.dot(key_grad_rows.reshape(-1, DK), key_proj.T, preferred_element_type=single)
        contribution = contribution + jnp.dot(value_grad_rows.reshape(-1, DK), value_proj.T, preferred_element_type=single)
        contribution = contribution + jnp.dot(query_grad.reshape(-1, DK), query_weight.T, preferred_element_type=single)
        contribution = contribution.astype(half)
        grad_sum = grad_sum.at[table_tok.reshape(-1)].add(contribution.astype(single))
        owned_single = owned_rows.astype(single)
        key_partial = jnp.einsum('crd,crk->cdk', owned_single, key_grad_rows.astype(single)).astype(half)
        value_partial = jnp.einsum('crd,crk->cdk', owned_single, value_grad_rows.astype(single)).astype(half)
        key_partial = lax.optimization_barrier(key_partial)
        value_partial = lax.optimization_barrier(value_partial)
        key_total = jnp.sum(key_partial.astype(single), axis=0)
        value_total = jnp.sum(value_partial.astype(single), axis=0)
        return grad_sum, (key_total, value_total)

    start_sum = jnp.zeros((TOKENS + 1, D), single)
    inputs = (token_table, pick_table, jnp.transpose(key_weight, (1, 0, 2)), jnp.transpose(value_weight, (1, 0, 2)), jnp.transpose(gates, (2, 0, 1)))
    grad_sum, stacked = lax.scan(one_memory, start_sum, inputs)
    token_grad = grad_sum[:TOKENS].astype(half)
    key_grad = jnp.transpose(stacked[0], (1, 0, 2))
    value_grad = jnp.transpose(stacked[1], (1, 0, 2))
    return (token_grad, key_grad, value_grad)
```

```python
import jax
import jax.numpy as jnp
from jax import lax
from jax.sharding import PartitionSpec as P


def shards(tokens, picks, route_weight, cotangent, query_weight, key_weight, value_weight, gates):
    half = jnp.bfloat16
    single = jnp.float32
    mem_count = lax.axis_size("mem")
    mem_local = key_weight.shape[1]
    mem_total = mem_count * mem_local
    tok_rows = tokens.shape[0]
    model_width = tokens.shape[1]
    head_width = query_weight.shape[1]
    capacity = 3 * tok_rows // mem_total
    query_rows = jnp.dot(tokens, query_weight, preferred_element_type=single).astype(half)
    weighted = (
        route_weight.astype(single)[:, :, None] * cotangent.astype(single)[:, None, :]
    ).astype(half)
    flat_ids = picks.reshape(-1)
    onehot = (flat_ids[:, None] == jnp.arange(mem_total, dtype=jnp.int32)[None, :]).astype(
        jnp.int32
    )
    before = jnp.cumsum(onehot, axis=0) - onehot
    slot_index = jnp.sum(before * onehot, axis=1)
    destination = flat_ids * capacity + slot_index
    pick_order = jnp.arange(2 * tok_rows, dtype=jnp.int32)
    token_table = (
        jnp.full((mem_total * capacity,), tok_rows, jnp.int32).at[destination].set(pick_order // 2)
    )
    pick_table = (
        jnp.full((mem_total * capacity,), 2 * tok_rows, jnp.int32).at[destination].set(pick_order)
    )
    padded_tokens = jnp.concatenate([tokens, jnp.zeros((1, model_width), half)], axis=0)
    pick_side = jnp.concatenate(
        [jnp.broadcast_to(query_rows[:, None, :], weighted.shape), weighted], axis=2
    )
    pick_side = jnp.concatenate(
        [pick_side.reshape(2 * tok_rows, 2 * head_width), jnp.zeros((1, 2 * head_width), half)],
        axis=0,
    )
    send_tokens = padded_tokens[token_table].reshape(mem_count, mem_local, capacity, model_width)
    send_side = pick_side[pick_table].reshape(mem_count, mem_local, capacity, 2 * head_width)
    got_tokens, got_side = (
        lax.all_to_all(send_tokens, "mem", split_axis=0, concat_axis=2, tiled=True),
        lax.all_to_all(send_side, "mem", split_axis=0, concat_axis=2, tiled=True),
    )
    owned_rows = got_tokens[0]
    owned_queries = got_side[0, :, :, :head_width]
    owned_weighted = got_side[0, :, :, head_width:]
    momentum = gates[0, 0]
    decay_multiplier = gates[0, 1]
    write_rate = gates[0, 2]
    everything = lax.all_gather(gates[0], "ctx", axis=0)
    group_count = lax.axis_size("ctx")
    piece = lax.all_gather(
        jnp.concatenate([key_weight, value_weight], axis=2), "ctx", axis=0, tiled=True
    )
    both = jnp.einsum("erd,dek->erk", owned_rows, piece, preferred_element_type=single).astype(half)
    key_rows = both[:, :, :head_width]
    value_rows = both[:, :, head_width:]
    written = write_rate[:, None, None] * jnp.einsum(
        "era,erb->eab", value_rows, key_rows, preferred_element_type=single
    )
    direct = jnp.einsum(
        "era,erb->eab", owned_weighted, owned_queries, preferred_element_type=single
    )
    slab = head_width // group_count
    payload = jnp.stack([written, direct]).astype(half)
    payload = payload.reshape(2, mem_local, group_count, slab, head_width).transpose(2, 0, 1, 3, 4)
    arrived = lax.all_to_all(payload, "ctx", split_axis=0, concat_axis=0, tiled=True).astype(single)
    factor = everything[:, 0, :, None, None]
    retain = everything[:, 1, :, None, None]
    rate = everything[:, 2, :, None, None]
    state = jnp.zeros_like(arrived[0, 0])
    memory = state
    memories = []
    for at in range(group_count):
        state = factor[at] * state + arrived[at, 0]
        memory = retain[at] * memory + state
        memories.append(memory.astype(half))
    carry_total = jnp.zeros_like(state)
    carry_adjoint = carry_total
    adjoints = []
    for at in range(group_count - 1, -1, -1):
        total = arrived[at, 1] + carry_total
        adjoint = total + carry_adjoint
        adjoints.append((rate[at] * adjoint).astype(half))
        carry_total = retain[at] * total
        carry_adjoint = factor[at] * adjoint
    back = jnp.stack([jnp.stack(memories), jnp.stack(adjoints[::-1])], axis=1)
    back = lax.all_to_all(back, "ctx", split_axis=0, concat_axis=0, tiled=True)
    back = back.transpose(1, 2, 0, 3, 4).reshape(2, mem_local, head_width, head_width)
    memory_half, scaled = back[0], back[1]
    query_grad = jnp.einsum(
        "era,eab->erb", owned_weighted, memory_half, preferred_element_type=single
    ).astype(half)
    value_grad_rows = jnp.einsum(
        "erb,eab->era", key_rows, scaled, preferred_element_type=single
    ).astype(half)
    key_grad_rows = jnp.einsum(
        "era,eab->erb", value_rows, scaled, preferred_element_type=single
    ).astype(half)
    grad_rows = jnp.concatenate([key_grad_rows, value_grad_rows], axis=2)
    columns = jnp.einsum("erk,dek->erd", grad_rows, piece, preferred_element_type=single)
    contribution = columns + jnp.einsum(
        "erk,dk->erd", query_grad, query_weight, preferred_element_type=single
    )
    returned = lax.all_to_all(
        contribution.astype(half)[None], "mem", split_axis=2, concat_axis=0, tiled=True
    )
    returned = returned.reshape(mem_total * capacity, model_width)
    token_grad = jnp.sum(
        returned[destination].reshape(tok_rows, 2, model_width).astype(single), axis=1
    ).astype(half)
    stacked_grads = jnp.stack([key_grad_rows, value_grad_rows], axis=2)
    rows_here = owned_rows
    shares = lax.psum_scatter(
        jnp.einsum(
            "erd,ersk->dsek", rows_here, stacked_grads, preferred_element_type=single
        ).astype(jnp.bfloat16),
        "ctx",
        scatter_dimension=0,
        tiled=True,
    ).astype(jnp.float32)
    return (token_grad, shares[:, 0], shares[:, 1])


def solution(mesh):
    return jax.shard_map(
        shards,
        mesh=mesh,
        in_specs=(
            P(("ctx", "mem"), None),
            P(("ctx", "mem"), None),
            P(("ctx", "mem"), None),
            P(("ctx", "mem"), None),
            P(),
            P("ctx", "mem", None),
            P("ctx", "mem", None),
            P("ctx", None, "mem"),
        ),
        out_specs=(P(("ctx", "mem"), None), P("ctx", "mem", None), P("ctx", "mem", None)),
        check_vma=False,
    )
```

```python
import jax
import jax.numpy as jnp
from jax import lax
from jax.experimental import pallas as pl
from jax.experimental.pallas import tpu as pltpu
from jax.sharding import PartitionSpec as P

MESH = pl.DeviceIdType.MESH
HALF = jnp.bfloat16
SINGLE = jnp.float32
TN = (((0,), (0,)), ((), ()))
NT = (((1,), (1,)), ((), ()))
NN = (((1,), (0,)), ((), ()))
OFFS_OUT = (0, 3, 1, 2)
OFFS_IN = (2, 1, 3, 0)


def dot(a, b, dims):
    return lax.dot_general(a, b, dims, preferred_element_type=SINGLE)


def kernel(
    tok, side, wloc, qw, gts,
    tg, kg, vg,
    T, W, QW, OWN, G, F1, R1, F2, R2, ACC, CS, RB, FW, XS, XR, PT,
    GB, SD, RD, SS, RSS, SW, RW, SM, RM, WT, KV, GR, QG,
    lsem, ws, wr, zs, zr, gas, gar, ds, dr, ss, sr, vs, vr, ms, mr, gs, gr, bs, br, fs, fr, xsem,
):
    c = lax.axis_index("ctx")
    m = lax.axis_index("mem")
    y, x = c // 4, c % 4
    z, k = m // 2, m % 2
    mate = m + 1 - 2 * k

    def mm(o, core):
        return ((z + o) % 4) * 2 + core

    pos = ((x, y), (y, x))

    def idx(e, p, s):
        return (s % 4) * 4 + p % 4 if e == 0 else (p % 4) * 4 + s % 4

    def to(e, dp, dsec):
        p, s = pos[e]
        return (idx(e, p + dp, s + dsec), m)

    def rc(src, dst, ssem, rsem, dev):
        return pltpu.make_async_remote_copy(
            src_ref=src, dst_ref=dst, send_sem=ssem, recv_sem=rsem,
            device_id=dev, device_id_type=MESH,
        )

    pending = []

    def send(src, dst, ssem, rsem, dev):
        d = rc(src, dst, ssem, rsem, dev)
        d.start()
        pending.append(d)

    def got(ref, ssem, rsem):
        rc(ref, ref, ssem, rsem, (c, mate)).wait_recv()

    locals_ = [
        pltpu.make_async_copy(tok, T.at[m, :, pl.ds(0, 4096)], lsem.at[0]),
        pltpu.make_async_copy(side, T.at[m, :, pl.ds(4096, 384)], lsem.at[1]),
        pltpu.make_async_copy(wloc.at[0], W.at[0, c], lsem.at[2]),
        pltpu.make_async_copy(wloc.at[1], W.at[1, c], lsem.at[3]),
        pltpu.make_async_copy(qw, QW, lsem.at[4]),
        pltpu.make_async_copy(gts, GB.at[c], lsem.at[5]),
    ]
    for d in locals_:
        d.start()

    barrier = pltpu.get_barrier_semaphore()

    def greet(off, _):
        pl.semaphore_signal(barrier, inc=1, device_id=((c + off) % 16, m), device_id_type=MESH)
        return 0

    lax.fori_loop(1, 16, greet, 0)
    for dev in (mate, mm(1, 0), mm(1, 1), mm(3, 0), mm(3, 1)):
        pl.semaphore_signal(barrier, inc=1, device_id=(c, dev), device_id_type=MESH)
    pl.semaphore_wait(barrier, 20)
    for d in locals_:
        d.wait()

    TOP, BOT = pl.ds(0, 64), pl.ds(64, 64)
    up, down, part = (c, mm(1, k)), (c, mm(3, k)), (c, mate)

    def zsend(slot, rows, n, dev):
        r = T.at[slot] if rows is None else T.at[slot, rows]
        send(r, r, zs.at[n], zr.at[n], dev)

    def zgot(slot, rows, n):
        got(T.at[slot] if rows is None else T.at[slot, rows], zs.at[n], zr.at[n])

    HT, HB = pl.ds(0, 128), pl.ds(128, 128)

    def wsend(e, block, rows, n, dp, dsec):
        r = W.at[e, block] if rows is None else W.at[e, block, rows]
        send(r, r, ws.at[e, n], wr.at[e, n], to(e, dp, dsec))

    def wgot(e, block, rows, n):
        got(W.at[e, block] if rows is None else W.at[e, block, rows], ws.at[e, n], wr.at[e, n])

    for e in range(2):
        wsend(e, c, None, 0, 1, 0)
        wsend(e, c, None, 1, -1 + 4, 0)
    zsend(m, TOP, 0, up)
    zsend(m, BOT, 1, down)
    zsend(m, BOT, 2, up)
    zsend(m, TOP, 3, down)
    zsend(m, None, 6, part)
    for e in range(2):
        wsend(e, c, None, 4, 0, 1)
        wsend(e, c, None, 5, 0, 3)

    def send_gate(off, _):
        there = (c + off) % 16
        rc(GB.at[c], GB.at[c], gas.at[off], gar.at[off], (there, m)).start()
        return 0

    lax.fori_loop(1, 16, send_gate, 0)

    def w_first(e):
        p, s = pos[e]
        b = idx(e, p + 3, s)
        wgot(e, b, None, 0)
        wsend(e, b, HT, 2, 1, 0)
        wsend(e, b, None, 8, 0, 1)
        wsend(e, b, None, 9, 0, 3)
        b = idx(e, p + 1, s)
        wgot(e, b, None, 1)
        wsend(e, b, HB, 3, 3, 0)
        wsend(e, b, None, 12, 0, 1)
        wsend(e, b, None, 13, 0, 3)

    def w_far(e):
        p, s = pos[e]
        b = idx(e, p + 2, s)
        wgot(e, b, HT, 2)
        wgot(e, b, HB, 3)
        wsend(e, b, None, 16, 0, 1)
        wsend(e, b, None, 17, 0, 3)

    def w_second(e, i):
        p, s = pos[e]
        b = idx(e, p + OFFS_OUT[i], s + 3)
        wgot(e, b, None, 4 + 4 * i)
        wsend(e, b, HT, 6 + 4 * i, 0, 1)
        b = idx(e, p + OFFS_OUT[i], s + 1)
        wgot(e, b, None, 5 + 4 * i)
        wsend(e, b, HB, 7 + 4 * i, 0, 3)

    def w_last(e, i):
        p, s = pos[e]
        b = idx(e, p + OFFS_OUT[i], s + 2)
        wgot(e, b, HT, 6 + 4 * i)
        wgot(e, b, HB, 7 + 4 * i)

    def positions(cols, core):
        n = cols.shape[0]
        p0, p1 = cols[:, 256:257].astype(SINGLE), cols[:, 257:258].astype(SINGLE)
        lane = lax.broadcasted_iota(jnp.int32, (n, 128), 1).astype(SINGLE)
        hits = jnp.where((lane == p0) | (lane == p1), 1.0, 0.0).astype(HALF)
        row = lax.broadcasted_iota(jnp.int32, (n, n), 0)
        col = lax.broadcasted_iota(jnp.int32, (n, n), 1)
        before = jnp.where((col < row) & (col // 128 == row // 128), 1.0, 0.0).astype(HALF)
        rank = dot(before, hits, NN)
        out = []
        for pk in (p0, p1):
            r = jnp.sum(jnp.where(lane == pk, rank, 0.0), axis=1, keepdims=True)
            out.append(48.0 * pk + 24.0 * core + r)
        return out

    blockrow = lax.broadcasted_iota(jnp.int32, (256, 1), 0) // 128
    mf = m.astype(SINGLE)
    kf = k.astype(SINGLE)

    def gather(o):
        zz = (z + o) % 4
        cols = T[pl.ds(2 * zz, 2), :, 4096:4480].reshape(256, 384)
        p0, p1 = positions(cols, blockrow.astype(SINGLE))
        lane = lax.broadcasted_iota(jnp.int32, (256, 128), 1)
        lf = lane.astype(SINGLE) + 96.0 * mf
        sel = jnp.where(((lf == p0) | (lf == p1)) & (lane < 96), 1.0, 0.0).astype(HALF)
        for a, n in ((0, 1024), (1024, 1024), (2048, 1024), (3072, 1024), (4096, 384)):
            picked = dot(sel, T[pl.ds(2 * zz, 2), :, a:a + n].reshape(256, n), TN).astype(HALF)
            OWN[0, zz, :, a:a + n] = picked[0:48]
            OWN[1, zz, :, a:a + n] = picked[48:96]

    def rows_of(e):
        return OWN[e, :, :, 0:4096].reshape(192, 4096)

    def exchange(src, dst, ssem, rsem):
        def one(off, _):
            there = (c + off) % 16
            rc(src.at[there], dst.at[c], ssem.at[off], rsem.at[off], (there, m)).start()
            return 0

        lax.fori_loop(1, 16, one, 0)
        dst[c] = src[c]

    def collect(dst, ssem, rsem):
        def one(off, _):
            rc(dst.at[0], dst.at[(c - off + 16) % 16], ssem.at[off], rsem.at[off], (c, mate)).wait_recv()
            return 0

        lax.fori_loop(1, 16, one, 0)

    def drain(src, ssem, rsem):
        def one(off, _):
            rc(src.at[0], src.at[0], ssem.at[off], rsem.at[off], (c, mate)).wait_send()
            return 0

        lax.fori_loop(1, 16, one, 0)

    def gate(at, which):
        g = GB[at]
        return jnp.concatenate(
            [jnp.broadcast_to(g[2 * which + e:2 * which + e + 1], (16, 256)) for e in range(2)], axis=0
        )

    w_first(0)
    w_first(1)
    zgot(mm(3, k), TOP, 0)
    zsend(mm(3, k), TOP, 4, up)
    zgot(mm(1, k), BOT, 1)
    zsend(mm(1, k), BOT, 5, down)
    w_far(0)
    w_far(1)
    zgot(m + 1 - 2 * k, None, 6)
    gather(0)
    own_cols = jnp.concatenate([T[m, :, 4096:4480], T[mate, :, 4096:4480]], axis=0)
    core = jnp.where(blockrow == 0, kf, 1.0 - kf)
    p0, p1 = positions(own_cols, core)
    lane = lax.broadcasted_iota(jnp.int32, (256, 768), 1).astype(SINGLE)
    PT[...] = jnp.where((lane == p0) | (lane == p1), 1.0, 0.0).astype(HALF)
    w_second(0, 0)
    w_second(1, 0)
    zgot(mm(3, k), BOT, 2)
    zsend(mm(3, k), None, 7, part)
    zgot(mm(1, k), TOP, 3)
    zsend(mm(1, k), None, 8, part)
    w_second(0, 1)
    w_second(1, 1)
    zgot(mm(3, 1 - k), None, 7)
    gather(3)
    w_second(0, 2)
    w_second(1, 2)
    zgot(mm(1, 1 - k), None, 8)
    gather(1)
    zgot(mm(2, k), TOP, 4)
    zgot(mm(2, k), BOT, 5)
    zsend(mm(2, k), None, 9, part)
    w_second(0, 3)
    w_second(1, 3)
    zgot(mm(2, 1 - k), None, 9)
    gather(2)

    for e in range(2):
        cols = OWN[e, :, :, 4096:4480].reshape(192, 384)
        mine = 2.0 * mf + e
        w = jnp.where(
            cols[:, 256:257].astype(SINGLE) == mine,
            cols[:, 258:259].astype(SINGLE),
            cols[:, 259:260].astype(SINGLE),
        )
        WT[e] = (w * cols[:, 0:256].astype(SINGLE)).astype(HALF)
        queries = dot(rows_of(e), QW[...], NN).astype(HALF)
        direct = dot(WT[e], queries, TN).astype(HALF)
        SD[:, 16 * e:16 * e + 16, :] = direct.reshape(16, 16, 256)
    exchange(SD, RD, ds, dr)
    collect(GB, gas, gar)
    collect(RD, ds, dr)

    def back(i, carry):
        at = 15 - i
        ct, ca = carry
        total = RD[at].astype(SINGLE) + ct
        adj = total + ca
        SS[at] = (gate(at, 2) * adj).astype(HALF)
        return gate(at, 1) * total, gate(at, 0) * adj

    zero = jnp.zeros((32, 256), SINGLE)
    lax.fori_loop(0, 16, back, (zero, zero))
    exchange(SS, RSS, ss, sr)

    for e in range(2):
        for i in range(4):
            w_last(e, i)
        KV[e] = dot(rows_of(e), W[e].reshape(4096, 512), NN).astype(HALF)
        written = dot(KV[e, :, 256:512], KV[e, :, 0:256], TN)
        written = GB[c, 4 + e:5 + e, :] * written
        SW[:, 16 * e:16 * e + 16, :] = written.astype(HALF).reshape(16, 16, 256)
    exchange(SW, RW, vs, vr)
    collect(RSS, ss, sr)
    for e in range(2):
        scaled = RSS[:, 16 * e:16 * e + 16, :].reshape(256, 256)
        GR[e, :, 0:256] = dot(KV[e, :, 256:512], scaled, NN).astype(HALF)
        GR[e, :, 256:512] = dot(KV[e, :, 0:256], scaled, NT).astype(HALF)

    def share(e, block):
        cols = OWN[e, :, :, pl.ds(pl.multiple_of(block * 256, 256), 256)].reshape(192, 256)
        G[e, block] = dot(cols, GR[e], TN).astype(HALF)

    def gsend(src, dst, e, n, dp, dsec):
        send(src, dst, gs.at[e, n], gr.at[e, n], to(e, dp, dsec))

    for i in range(4):
        for e in range(2):
            p, s = pos[e]
            b = idx(e, p + OFFS_IN[i], s + 2)
            share(e, b)
            gsend(G.at[e, b, HT], F1.at[e, i, 0], e, 4 * i, 0, 1)
            gsend(G.at[e, b, HB], F1.at[e, i, 1], e, 4 * i + 1, 0, 3)

    def rest(q, _):
        for e in range(2):
            p, s = pos[e]
            for o in (1, 3, 0):
                share(e, idx(e, q, s + o))
        return 0

    collect(RW, vs, vr)

    def forth(at, carry):
        state, memory = carry
        state = gate(at, 0) * state + RW[at].astype(SINGLE)
        memory = gate(at, 1) * memory + state
        SM[at] = memory.astype(HALF)
        return state, memory

    lax.fori_loop(0, 16, forth, (zero, zero))
    exchange(SM, RM, ms, mr)
    lax.fori_loop(0, 4, rest, 0)

    def add_rows(dst, parts, start, rows, out=None):
        def one(i, _):
            r = pl.ds(pl.multiple_of(start + i * 32, 32), 32)
            total = dst[r, :].astype(SINGLE)
            for ref, base in parts:
                total = total + ref[pl.ds(pl.multiple_of(base + i * 32, 32), 32), :].astype(SINGLE)
            if out is None:
                dst[r, :] = total.astype(HALF)
            else:
                out[r, :] = total
            return 0

        lax.fori_loop(0, rows // 32, one, 0)

    def r_first(e, i):
        p, s = pos[e]
        b = idx(e, p + OFFS_IN[i], s + 1)
        got(F1.at[e, i, 0], gs.at[e, 4 * i], gr.at[e, 4 * i])
        add_rows(G.at[e, b], [(F1.at[e, i, 0], 0)], 0, 128)
        gsend(G.at[e, b], R1.at[e, i, 0], e, 4 * i + 2, 0, 1)
        b = idx(e, p + OFFS_IN[i], s + 3)
        got(F1.at[e, i, 1], gs.at[e, 4 * i + 1], gr.at[e, 4 * i + 1])
        add_rows(G.at[e, b], [(F1.at[e, i, 1], 0)], 128, 128)
        gsend(G.at[e, b], R1.at[e, i, 1], e, 4 * i + 3, 0, 3)

    def r_sum(e, i):
        p, s = pos[e]
        b = idx(e, p + OFFS_IN[i], s)
        got(R1.at[e, i, 0], gs.at[e, 4 * i + 2], gr.at[e, 4 * i + 2])
        got(R1.at[e, i, 1], gs.at[e, 4 * i + 3], gr.at[e, 4 * i + 3])
        add_rows(
            G.at[e, b], [(R1.at[e, i, 0], 0), (R1.at[e, i, 1], 0)], 0, 256,
            ACC.at[e] if i == 3 else None,
        )
        if i == 0:
            gsend(G.at[e, b, HT], F2.at[e, 0], e, 16, 1, 0)
            gsend(G.at[e, b, HB], F2.at[e, 1], e, 17, 3, 0)

    def r_pass(e, i):
        p, s = pos[e]
        b = idx(e, p + OFFS_IN[i], s)
        got(F2.at[e, i - 1], gs.at[e, 15 + i], gr.at[e, 15 + i])
        add_rows(G.at[e, b], [(F2.at[e, i - 1], 0)], 128 * (i - 1), 128)
        gsend(G.at[e, b], R2.at[e, i - 1], e, 17 + i, 1 if i == 1 else 3, 0)

    r_first(0, 0)
    r_first(1, 0)

    collect(RM, ms, mr)
    for e in range(2):
        memory = RM[:, 16 * e:16 * e + 16, :].reshape(256, 256)
        QG[e] = dot(WT[e], memory, NN).astype(HALF)

    H0, H1 = pl.ds(0, 48), pl.ds(48, 48)

    def bsend(src, dst, ssem, slot, part_, dev):
        send(src, dst, ssem, br.at[slot, part_], (c, dev))

    far, near, below = (z + 2) % 4, (z + 1) % 4, (z + 3) % 4
    for h in range(2):
        def column(i, _, h=h):
            for e in range(2):
                block = 8 * h + i
                out = dot(GR[e], W[e, block], NT)
                out = out + dot(QG[e], QW[pl.ds(pl.multiple_of(block * 256, 256), 256), :], NT)
                CS[h, :, 48 * e:48 * e + 48, pl.ds(pl.multiple_of(i * 256, 256), 256)] = (
                    out.astype(HALF).reshape(4, 48, 256)
                )
            return 0

        lax.fori_loop(0, 8, column, 0)
        send(CS.at[h, far, H0], FW.at[0, h], fs.at[0, h], fr.at[0, h], up)
        send(CS.at[h, far, H1], FW.at[1, h], fs.at[1, h], fr.at[1, h], down)
        bsend(CS.at[h, near], RB.at[m], bs.at[h, 0], m, 0, mm(1, h))
        bsend(CS.at[h, below], RB.at[m], bs.at[h, 1], m, 0, mm(3, h))
    bsend(CS.at[1 - k, z], RB.at[m], bs.at[0, 4], m, 0, mate)
    RB[m] = CS[k, z]

    r_first(0, 1)
    r_first(1, 1)
    r_first(0, 2)
    r_first(1, 2)
    for h in range(2):
        got(FW.at[0, h], fs.at[0, h], fr.at[0, h])
        bsend(FW.at[0, h], RB.at[mm(3, k), H0], bs.at[h, 2], mm(3, k), 0, mm(1, h))
        got(FW.at[1, h], fs.at[1, h], fr.at[1, h])
        bsend(FW.at[1, h], RB.at[mm(1, k), H1], bs.at[h, 3], mm(1, k), 1, mm(3, h))
    r_first(0, 3)
    r_first(1, 3)
    for i in range(3):
        for e in range(2):
            r_sum(e, i)
    for i in (1, 2):
        for e in range(2):
            r_pass(e, i)
    for e in range(2):
        r_sum(e, 3)

    got(RB.at[mate], bs.at[0, 4], br.at[mate, 0])
    for h in range(2):
        got(RB.at[mm(1, h)], bs.at[0, 0], br.at[mm(1, h), 0])
        got(RB.at[mm(3, h)], bs.at[0, 0], br.at[mm(3, h), 0])
        got(RB.at[mm(2, h), H0], bs.at[0, 0], br.at[mm(2, h), 0])
        got(RB.at[mm(2, h), H1], bs.at[0, 0], br.at[mm(2, h), 1])

    mycols = pl.multiple_of(k * 2048, 2048)
    matecols = pl.multiple_of((1 - k) * 2048, 2048)

    def combine(i, _):
        n = pl.ds(pl.multiple_of(i * 512, 512), 512)
        total = dot(PT[...], RB[:, :, n].reshape(768, 512), NN).astype(HALF)
        XS[:, n] = total[128:256]
        tg[:, pl.ds(pl.multiple_of(mycols + i * 512, 512), 512)] = total[0:128]
        return 0

    lax.fori_loop(0, 4, combine, 0)
    send(XS, XR, xsem.at[0], xsem.at[1], part)

    for e in range(2):
        got(R2.at[e, 0], gs.at[e, 18], gr.at[e, 18])
        got(R2.at[e, 1], gs.at[e, 19], gr.at[e, 19])

        def final(i, _, e=e):
            r = pl.ds(pl.multiple_of(i * 32, 32), 32)
            total = ACC[e, r, :] + R2[e, 0, r, :].astype(SINGLE) + R2[e, 1, r, :].astype(SINGLE)
            kg[r, 256 * e:256 * e + 256] = total[:, 0:256]
            vg[r, 256 * e:256 * e + 256] = total[:, 256:512]
            return 0

        lax.fori_loop(0, 8, final, 0)
    got(XR, xsem.at[0], xsem.at[1])
    tg[:, pl.ds(matecols, 2048)] = XR[...]

    for d in pending:
        d.wait_send()
    drain(GB, gas, gar)
    drain(SD, ds, dr)
    drain(SS, ss, sr)
    drain(SW, vs, vr)
    drain(SM, ms, mr)


def shards(tokens, picks, route_weight, cotangent, query_weight, key_weight, value_weight, gates):
    side = jnp.concatenate(
        [cotangent, picks.astype(HALF), route_weight, jnp.zeros((128, 124), HALF)], axis=1
    )
    wloc = jnp.concatenate([key_weight, value_weight], axis=2).transpose(1, 0, 2)
    gts = jnp.broadcast_to(gates.reshape(6, 1), (6, 256))
    gts = jnp.concatenate([gts, jnp.zeros((2, 256), SINGLE)], axis=0)
    anywhere = pl.BlockSpec(memory_space=pl.ANY)
    vmem = pl.BlockSpec(memory_space=pltpu.VMEM)
    V = pltpu.VMEM
    S = pltpu.SemaphoreType.DMA
    tg, kg, vg = pl.pallas_call(
        kernel,
        out_shape=(
            jax.ShapeDtypeStruct((128, 4096), HALF),
            jax.ShapeDtypeStruct((256, 512), SINGLE),
            jax.ShapeDtypeStruct((256, 512), SINGLE),
        ),
        in_specs=[anywhere, anywhere, anywhere, anywhere, anywhere],
        out_specs=(vmem, vmem, vmem),
        scratch_shapes=[
            V((8, 128, 4480), HALF),
            V((2, 16, 256, 512), HALF),
            V((4096, 256), HALF),
            V((2, 4, 48, 4480), HALF),
            V((2, 16, 256, 512), HALF),
            V((2, 4, 2, 128, 512), HALF),
            V((2, 4, 2, 256, 512), HALF),
            V((2, 2, 128, 512), HALF),
            V((2, 2, 256, 512), HALF),
            V((2, 256, 512), SINGLE),
            V((2, 4, 96, 2048), HALF),
            V((8, 96, 2048), HALF),
            V((2, 2, 48, 2048), HALF),
            V((128, 2048), HALF),
            V((128, 2048), HALF),
            V((256, 768), HALF),
            V((16, 8, 256), SINGLE),
        ]
        + [V((16, 32, 256), HALF)] * 8
        + [
            V((2, 192, 256), HALF),
            V((2, 192, 512), HALF),
            V((2, 192, 512), HALF),
            V((2, 192, 256), HALF),
            S((6,)),
            S((2, 20)), S((2, 20)),
            S((10,)), S((10,)),
            S((16,)), S((16,)),
            S((16,)), S((16,)),
            S((16,)), S((16,)),
            S((16,)), S((16,)),
            S((16,)), S((16,)),
            S((2, 20)), S((2, 20)),
            S((2, 5)), S((8, 2)),
            S((2, 2)), S((2, 2)),
            S((2,)),
        ],
        compiler_params=pltpu.CompilerParams(
            collective_id=0, has_side_effects=True, vmem_limit_bytes=60 * 1024 * 1024
        ),
    )(tokens, side, wloc, query_weight, gts)
    return tg, kg.reshape(256, 2, 256), vg.reshape(256, 2, 256)


def solution(mesh):
    return jax.shard_map(
        shards,
        mesh=mesh,
        in_specs=(
            P(("ctx", "mem"), None),
            P(("ctx", "mem"), None),
            P(("ctx", "mem"), None),
            P(("ctx", "mem"), None),
            P(),
            P("ctx", "mem", None),
            P("ctx", "mem", None),
            P("ctx", None, "mem"),
        ),
        out_specs=(P(("ctx", "mem"), None), P("ctx", "mem", None), P("ctx", "mem", None)),
        check_vma=False,
    )
```

```python
import jax
import jax.numpy as jnp
from jax import lax
from jax.experimental import pallas as pl
from jax.experimental.pallas import tpu as pltpu
from jax.sharding import PartitionSpec as P

MESH = pl.DeviceIdType.MESH
HALF = jnp.bfloat16
SINGLE = jnp.float32
TN = (((0,), (0,)), ((), ()))
NT = (((1,), (1,)), ((), ()))
NN = (((1,), (0,)), ((), ()))
OFFS_OUT = (0, 3, 1, 2)
OFFS_IN = (2, 1, 3, 0)


def dot(a, b, dims):
    return lax.dot_general(a, b, dims, preferred_element_type=SINGLE)


def kernel(
    tok, picks, weight, cot, qw, kw, vw, gates,
    tg, kg, vg,
    T, SIDE, MT, W, QW, OWN, SELT, QS, G, F1, R1, F2, R2, ACC, CS, RB, XS, XR, PT, QGS, QGR, BASE, KVA,
    GB, SD, RD, SS, RSS, SW, RW, SM, RM, WT, KV, GR,
    lsem, ws, wr, zs, zr, es, er, hs, hr, gas, gar, ds, dr, ss, sr, vs, vr, ms, mr, gs, gr, bs, br, qs, qr, xs, xr,
):
    c = lax.axis_index("ctx")
    m = lax.axis_index("mem")
    y, x = c // 4, c % 4
    z, k = m // 2, m % 2
    mate = m + 1 - 2 * k

    def mm(o, core):
        return ((z + o) % 4) * 2 + core

    pos = ((x, y), (y, x))

    def idx(e, p, s):
        return (s % 4) * 4 + p % 4 if e == 0 else (p % 4) * 4 + s % 4

    def to(e, dp, dsec):
        p, s = pos[e]
        return (idx(e, p + dp, s + dsec), m)

    def rc(src, dst, ssem, rsem, dev):
        return pltpu.make_async_remote_copy(
            src_ref=src, dst_ref=dst, send_sem=ssem, recv_sem=rsem,
            device_id=dev, device_id_type=MESH,
        )

    pending = []

    def send(src, dst, ssem, rsem, dev):
        d = rc(src, dst, ssem, rsem, dev)
        d.start()
        pending.append(d)

    def got(ref, ssem, rsem):
        rc(ref, ref, ssem, rsem, (c, mate)).wait_recv()

    locals_ = [
        pltpu.make_async_copy(tok, T.at[m], lsem.at[0]),
        pltpu.make_async_copy(qw, QW, lsem.at[1]),
        pltpu.make_async_copy(cot, SIDE.at[m, :, pl.ds(0, 256)], lsem.at[2]),
    ]
    for d in locals_:
        d.start()

    barrier = pltpu.get_barrier_semaphore()

    def greet(off, _):
        pl.semaphore_signal(barrier, inc=1, device_id=((c + off) % 16, m), device_id_type=MESH)
        return 0

    def greet_mem(off, _):
        pl.semaphore_signal(barrier, inc=1, device_id=(c, (m + off) % 8), device_id_type=MESH)
        return 0

    lax.fori_loop(1, 16, greet, 0)
    lax.fori_loop(1, 8, greet_mem, 0)
    for e in range(2):
        W[e, c, :, 0:256] = kw[:, e, :]
        W[e, c, :, 256:512] = vw[:, e, :]
        for g in range(3):
            GB[c, 2 * g + e:2 * g + e + 1, :] = jnp.full((1, 256), gates[e, g], SINGLE)
    GB[c, 6:8, :] = jnp.zeros((2, 256), SINGLE)
    MT[m] = jnp.concatenate(
        [picks[...].astype(SINGLE), weight[...].astype(SINGLE), jnp.zeros((4, 128), SINGLE)], axis=0
    )
    pl.semaphore_wait(barrier, 22)

    TOP, BOT = pl.ds(0, 64), pl.ds(64, 64)
    up, down, part = (c, mm(1, k)), (c, mm(3, k)), (c, mate)

    def zsend(buf, sems, slot, rows, n, dev):
        r = buf.at[slot] if rows is None else buf.at[slot, rows]
        send(r, r, sems[0].at[n], sems[1].at[n], dev)

    def zgot(buf, sems, slot, rows, n):
        got(buf.at[slot] if rows is None else buf.at[slot, rows], sems[0].at[n], sems[1].at[n])

    tz, ez = (zs, zr), (es, er)

    def z_start(buf, sems):
        zsend(buf, sems, m, TOP, 0, up)
        zsend(buf, sems, m, BOT, 1, down)
        zsend(buf, sems, m, BOT, 2, up)
        zsend(buf, sems, m, TOP, 3, down)
        zsend(buf, sems, m, None, 6, part)

    def z_forward(buf, sems):
        zgot(buf, sems, mm(3, k), TOP, 0)
        zsend(buf, sems, mm(3, k), TOP, 4, up)
        zgot(buf, sems, mm(1, k), BOT, 1)
        zsend(buf, sems, mm(1, k), BOT, 5, down)

    def z_hand(buf, sems):
        zgot(buf, sems, mm(3, k), BOT, 2)
        zsend(buf, sems, mm(3, k), None, 7, part)
        zgot(buf, sems, mm(1, k), TOP, 3)
        zsend(buf, sems, mm(1, k), None, 8, part)

    def z_far(buf, sems):
        zgot(buf, sems, mm(2, k), TOP, 4)
        zsend(buf, sems, mm(2, k), TOP, 9, part)
        zgot(buf, sems, mm(2, k), BOT, 5)
        zsend(buf, sems, mm(2, k), BOT, 10, part)

    def z_mate(buf, sems, o):
        if o == 2:
            zgot(buf, sems, mm(2, 1 - k), TOP, 9)
            zgot(buf, sems, mm(2, 1 - k), BOT, 10)
        else:
            zgot(buf, sems, mm(o, 1 - k), None, {0: 6, 3: 7, 1: 8}[o])

    HT, HB = pl.ds(0, 128), pl.ds(128, 128)

    def wsend(e, block, rows, n, dp, dsec):
        r = W.at[e, block] if rows is None else W.at[e, block, rows]
        send(r, r, ws.at[e, n], wr.at[e, n], to(e, dp, dsec))

    def wgot(e, block, rows, n):
        got(W.at[e, block] if rows is None else W.at[e, block, rows], ws.at[e, n], wr.at[e, n])

    def send_gate(off, _):
        there = (c + off) % 16
        rc(GB.at[c], GB.at[c], gas.at[off], gar.at[off], (there, m)).start()
        return 0

    def send_meta(off, _):
        there = (m + off) % 8
        rc(MT.at[m], MT.at[m], hs.at[off], hr.at[off], (c, there)).start()
        return 0

    lax.fori_loop(1, 8, send_meta, 0)
    lax.fori_loop(1, 16, send_gate, 0)
    for e in range(2):
        wsend(e, c, None, 0, 1, 0)
        wsend(e, c, None, 1, 3, 0)
    for e in range(2):
        wsend(e, c, None, 4, 0, 1)
        wsend(e, c, None, 5, 0, 3)
    for d in locals_:
        d.wait()
    SIDE[m, :, 256:512] = dot(T[m], QW[...], NN).astype(HALF)
    zsend(SIDE, ez, m, None, 2, (c, mm(2, k)))
    zsend(SIDE, ez, m, None, 0, up)
    zsend(SIDE, ez, m, None, 1, down)
    zsend(SIDE, ez, m, None, 6, part)
    z_start(T, tz)

    def side_hand(o):
        n = {3: 0, 1: 1, 2: 2}[o]
        zgot(SIDE, ez, mm(o, k), None, n)
        zsend(SIDE, ez, mm(o, k), None, 7 + n, part)

    def side_mate(o):
        zgot(SIDE, ez, mm(o, 1 - k), None, {0: 6, 3: 7, 1: 8, 2: 9}[o])

    def w_first(e):
        p, s = pos[e]
        b = idx(e, p + 3, s)
        wgot(e, b, None, 0)
        wsend(e, b, HT, 2, 1, 0)
        b = idx(e, p + 1, s)
        wgot(e, b, None, 1)
        wsend(e, b, HB, 3, 3, 0)

    def w_spread(e, i):
        p, s = pos[e]
        b = idx(e, p + OFFS_OUT[i], s)
        wsend(e, b, None, 4 + 4 * i, 0, 1)
        wsend(e, b, None, 5 + 4 * i, 0, 3)

    def w_far(e):
        p, s = pos[e]
        b = idx(e, p + 2, s)
        wgot(e, b, HT, 2)
        wgot(e, b, HB, 3)

    def w_second(e, i):
        p, s = pos[e]
        b = idx(e, p + OFFS_OUT[i], s + 3)
        wgot(e, b, None, 4 + 4 * i)
        wsend(e, b, HT, 6 + 4 * i, 0, 1)
        b = idx(e, p + OFFS_OUT[i], s + 1)
        wgot(e, b, None, 5 + 4 * i)
        wsend(e, b, HB, 7 + 4 * i, 0, 3)

    def w_last(e, i):
        p, s = pos[e]
        b = idx(e, p + OFFS_OUT[i], s + 2)
        wgot(e, b, HT, 6 + 4 * i)
        wgot(e, b, HB, 7 + 4 * i)

    sub = lax.broadcasted_iota(jnp.int32, (128, 128), 0)
    lane = lax.broadcasted_iota(jnp.int32, (128, 128), 1)
    before = jnp.where(sub < lane, 1.0, 0.0).astype(HALF)
    subf = sub.astype(SINGLE)
    mf = m.astype(SINGLE)

    def positions(d, core):
        meta = MT[d]
        p0, p1 = meta[0:1], meta[1:2]
        hits = jnp.where((subf == p0) | (subf == p1), 1.0, 0.0).astype(HALF)
        rank = dot(hits, before, NN)
        out = []
        for pk in (p0, p1):
            r = jnp.sum(jnp.where(subf == pk, rank, 0.0), axis=0, keepdims=True)
            out.append(48.0 * pk + 24.0 * core + r)
        return out

    def gather_side(o):
        zz = (z + o) % 4
        ws_, sels = [], []
        for core in range(2):
            p0, p1 = positions(2 * zz + core, float(core))
            at = subf + 96.0 * mf
            sel = jnp.where(((at == p0) | (at == p1)) & (sub < 96), 1.0, 0.0)
            meta = MT[2 * zz + core]
            w = []
            for e in range(2):
                pick = jnp.where(meta[0:1] == 2.0 * mf + e, meta[2:3], meta[3:4])
                w.append(jnp.sum(sel[48 * e:48 * e + 48] * pick, axis=1, keepdims=True))
            ws_.append(w)
            sels.append(sel.astype(HALF))
        sel = jnp.concatenate(sels, axis=1)
        SELT[zz] = sel
        got_side = dot(sel, SIDE[pl.ds(2 * zz, 2)].reshape(256, 512), NN)
        for e in range(2):
            w = ws_[0][e] + ws_[1][e]
            rows = got_side[48 * e:48 * e + 48]
            WT[e, zz] = (w * rows[:, 0:256]).astype(HALF)
            QS[e, zz] = rows[:, 256:512].astype(HALF)

    def gather(o):
        zz = (z + o) % 4
        for a in range(0, 4096, 1024):
            picked = dot(SELT[zz], T[pl.ds(2 * zz, 2), :, a:a + 1024].reshape(256, 1024), NN).astype(HALF)
            OWN[0, zz, :, a:a + 1024] = picked[0:48]
            OWN[1, zz, :, a:a + 1024] = picked[48:96]

    def exchange(src, dst, ssem, rsem):
        def one(off, _):
            there = (c + off) % 16
            rc(src.at[there], dst.at[c], ssem.at[off], rsem.at[off], (there, m)).start()
            return 0

        lax.fori_loop(1, 16, one, 0)
        dst[c] = src[c]

    def collect(dst, ssem, rsem):
        def one(off, _):
            rc(dst.at[0], dst.at[(c - off + 16) % 16], ssem.at[off], rsem.at[off], (c, mate)).wait_recv()
            return 0

        lax.fori_loop(1, 16, one, 0)

    def drain(src, ssem, rsem):
        def one(off, _):
            rc(src.at[0], src.at[0], ssem.at[off], rsem.at[off], (c, mate)).wait_send()
            return 0

        lax.fori_loop(1, 16, one, 0)

    def collect_mem(dst, ssem, rsem):
        def one(off, _):
            rc(dst.at[0], dst.at[(m - off + 8) % 8], ssem.at[off], rsem.at[off], (c, mate)).wait_recv()
            return 0

        lax.fori_loop(1, 8, one, 0)

    def drain_mem(src, ssem, rsem):
        def one(off, _):
            rc(src.at[0], src.at[0], ssem.at[off], rsem.at[off], (c, mate)).wait_send()
            return 0

        lax.fori_loop(1, 8, one, 0)

    def gate(at, which):
        g = GB[at]
        return jnp.concatenate(
            [jnp.broadcast_to(g[2 * which + e:2 * which + e + 1], (16, 256)) for e in range(2)], axis=0
        )

    def kv_part(e, i):
        p, s = pos[e]
        total = KVA[e] if i else jnp.zeros((192, 512), SINGLE)
        for o in range(4):
            b = idx(e, p + OFFS_OUT[i], s + o)
            cols = OWN[e, :, :, pl.ds(pl.multiple_of(b * 256, 256), 256)].reshape(192, 256)
            total = total + dot(cols, W[e, b], NN)
        if i < 3:
            KVA[e] = total
        else:
            KV[e] = total.astype(HALF)

    def back(i, carry):
        at = 15 - i
        ct, ca = carry
        total = RD[at].astype(SINGLE) + ct
        adj = total + ca
        SS[at] = (gate(at, 2) * adj).astype(HALF)
        return gate(at, 1) * total, gate(at, 0) * adj

    zero = jnp.zeros((32, 256), SINGLE)
    w_first(0)
    w_first(1)
    for o in (3, 1, 2):
        side_hand(o)
    collect_mem(MT, hs, hr)
    for o in (0, 3, 1, 2):
        side_mate(o)
        gather_side(o)
    for e in range(2):
        direct = dot(WT[e].reshape(192, 256), QS[e].reshape(192, 256), TN).astype(HALF)
        SD[:, 16 * e:16 * e + 16, :] = direct.reshape(16, 16, 256)
    exchange(SD, RD, ds, dr)
    w_spread(0, 1)
    w_spread(1, 1)
    z_mate(T, tz, 0)
    gather(0)
    w_far(0)
    w_far(1)
    collect(GB, gas, gar)
    collect(RD, ds, dr)
    lax.fori_loop(0, 16, back, (zero, zero))
    exchange(SS, RSS, ss, sr)
    for i in (2, 3):
        for e in range(2):
            w_spread(e, i)
    z_forward(T, tz)
    w_second(0, 0)
    w_second(1, 0)
    rows768 = lax.broadcasted_iota(jnp.int32, (768, 128), 0).astype(SINGLE)
    kf = k.astype(SINGLE)
    for half, (d, core) in enumerate(((m, kf), (mate, 1.0 - kf))):
        p0, p1 = positions(d, core)
        hot = jnp.where((rows768 == p0) | (rows768 == p1), 1.0, 0.0)
        PT[128 * half:128 * half + 128, :] = hot.T.astype(HALF)
    w_second(0, 1)
    w_second(1, 1)
    w_second(0, 2)
    w_second(1, 2)
    z_hand(T, tz)
    z_mate(T, tz, 3)
    gather(3)
    w_second(0, 3)
    w_second(1, 3)
    z_mate(T, tz, 1)
    gather(1)
    collect(RSS, ss, sr)
    z_far(T, tz)
    z_mate(T, tz, 2)
    gather(2)

    for i in range(4):
        for e in range(2):
            w_last(e, i)
            kv_part(e, i)
    for e in range(2):
        written = dot(KV[e, :, 256:512], KV[e, :, 0:256], TN)
        written = GB[c, 4 + e:5 + e, :] * written
        SW[:, 16 * e:16 * e + 16, :] = written.astype(HALF).reshape(16, 16, 256)
    exchange(SW, RW, vs, vr)
    for e in range(2):
        scaled = RSS[:, 16 * e:16 * e + 16, :].reshape(256, 256)
        GR[e, :, 0:256] = dot(KV[e, :, 256:512], scaled, NN).astype(HALF)
        GR[e, :, 256:512] = dot(KV[e, :, 0:256], scaled, NT).astype(HALF)

    def share(e, block):
        cols = OWN[e, :, :, pl.ds(pl.multiple_of(block * 256, 256), 256)].reshape(192, 256)
        G[e, block] = dot(cols, GR[e], TN).astype(HALF)

    def gsend(src, dst, e, n, dp, dsec):
        send(src, dst, gs.at[e, n], gr.at[e, n], to(e, dp, dsec))

    def g_start(e, i):
        p, s = pos[e]
        b = idx(e, p + OFFS_IN[i], s + 2)
        share(e, b)
        gsend(G.at[e, b, HT], F1.at[e, i, 0], e, 4 * i, 0, 1)
        gsend(G.at[e, b, HB], F1.at[e, i, 1], e, 4 * i + 1, 0, 3)

    for i in (0, 1):
        for e in range(2):
            g_start(e, i)

    def rest(q, _):
        for e in range(2):
            p, s = pos[e]
            for o in (1, 3, 0):
                share(e, idx(e, q, s + o))
        return 0

    def forth(at, carry):
        state, memory = carry
        state = gate(at, 0) * state + RW[at].astype(SINGLE)
        memory = gate(at, 1) * memory + state
        SM[at] = memory.astype(HALF)
        return state, memory

    def add_rows(dst, parts, start, rows, out=None):
        def one(i, _):
            r = pl.ds(pl.multiple_of(start + i * 32, 32), 32)
            total = dst[r, :].astype(SINGLE)
            for ref, base in parts:
                total = total + ref[pl.ds(pl.multiple_of(base + i * 32, 32), 32), :].astype(SINGLE)
            if out is None:
                dst[r, :] = total.astype(HALF)
            else:
                out[r, :] = total
            return 0

        lax.fori_loop(0, rows // 32, one, 0)

    def r_first(e, i):
        p, s = pos[e]
        b = idx(e, p + OFFS_IN[i], s + 1)
        got(F1.at[e, i, 0], gs.at[e, 4 * i], gr.at[e, 4 * i])
        add_rows(G.at[e, b], [(F1.at[e, i, 0], 0)], 0, 128)
        gsend(G.at[e, b], R1.at[e, i, 0], e, 4 * i + 2, 0, 1)
        b = idx(e, p + OFFS_IN[i], s + 3)
        got(F1.at[e, i, 1], gs.at[e, 4 * i + 1], gr.at[e, 4 * i + 1])
        add_rows(G.at[e, b], [(F1.at[e, i, 1], 0)], 128, 128)
        gsend(G.at[e, b], R1.at[e, i, 1], e, 4 * i + 3, 0, 3)

    def r_sum(e, i):
        p, s = pos[e]
        b = idx(e, p + OFFS_IN[i], s)
        got(R1.at[e, i, 0], gs.at[e, 4 * i + 2], gr.at[e, 4 * i + 2])
        got(R1.at[e, i, 1], gs.at[e, 4 * i + 3], gr.at[e, 4 * i + 3])
        add_rows(
            G.at[e, b], [(R1.at[e, i, 0], 0), (R1.at[e, i, 1], 0)], 0, 256,
            ACC.at[e] if i == 3 else None,
        )
        if i == 0:
            gsend(G.at[e, b, HT], F2.at[e, 0], e, 16, 1, 0)
            gsend(G.at[e, b, HB], F2.at[e, 1], e, 17, 3, 0)

    def r_pass(e, i):
        p, s = pos[e]
        b = idx(e, p + OFFS_IN[i], s)
        got(F2.at[e, i - 1], gs.at[e, 15 + i], gr.at[e, 15 + i])
        add_rows(G.at[e, b], [(F2.at[e, i - 1], 0)], 128 * (i - 1), 128)
        gsend(G.at[e, b], R2.at[e, i - 1], e, 17 + i, 1 if i == 1 else 3, 0)

    def bsend(src, n, slot, dev):
        send(src, RB.at[slot], bs.at[n], br.at[slot], (c, dev))

    def contribute(h):
        def column(i, _):
            for e in range(2):
                out = dot(GR[e], W[e, 8 * h + i], NT)
                CS[h, :, 48 * e:48 * e + 48, pl.ds(pl.multiple_of(i * 256, 256), 256)] = (
                    out.astype(HALF).reshape(4, 48, 256)
                )
            return 0

        lax.fori_loop(0, 8, column, 0)

    def dispatch(h):
        for o in (2, 1, 3):
            bsend(CS.at[h, (z + o) % 4], 4 * h + o, m, mm(o, h))

    contribute(0)
    dispatch(0)
    collect(RW, vs, vr)
    lax.fori_loop(0, 16, forth, (zero, zero))
    exchange(SM, RM, ms, mr)
    for i in (2, 3):
        for e in range(2):
            g_start(e, i)
    lax.fori_loop(0, 4, rest, 0)
    r_first(0, 0)
    r_first(1, 0)
    contribute(1)
    r_first(0, 1)
    r_first(1, 1)

    collect(RM, ms, mr)
    for e in range(2):
        memory = RM[:, 16 * e:16 * e + 16, :].reshape(256, 256)
        grad = dot(WT[e].reshape(192, 256), memory, NN).astype(HALF)
        QGS[:, 48 * e:48 * e + 48, :] = grad.reshape(4, 48, 256)

    def send_query(off, _):
        there = (m + off) % 8
        rc(QGS.at[there // 2], QGR.at[m], qs.at[off], qr.at[off], (c, there)).start()
        return 0

    lax.fori_loop(1, 8, send_query, 0)
    QGR[m] = QGS[z]
    dispatch(1)
    bsend(CS.at[1 - k, z], 0, m, mate)
    RB[m] = CS[k, z]

    r_first(0, 2)
    r_first(1, 2)
    r_first(0, 3)
    r_first(1, 3)
    r_sum(0, 0)
    r_sum(1, 0)
    r_sum(0, 1)
    r_sum(1, 1)
    r_pass(0, 1)
    r_pass(1, 1)
    r_sum(0, 2)
    r_sum(1, 2)
    r_pass(0, 2)
    r_pass(1, 2)
    collect_mem(QGR, qs, qr)
    grads = dot(PT[...], QGR[...].reshape(768, 256), NN).astype(HALF)

    def base(i, _):
        n = pl.multiple_of(i * 512, 512)
        BASE[:, pl.ds(n, 512)] = dot(grads, QW[pl.ds(pl.multiple_of(k * 2048 + n, 512), 512), :], NT)
        return 0

    lax.fori_loop(0, 4, base, 0)
    r_sum(0, 3)
    r_sum(1, 3)

    def arrived(off, _):
        there = (m + off) % 8
        rc(RB.at[0], RB.at[there], bs.at[0], br.at[there], (c, mate)).wait_recv()
        return 0

    lax.fori_loop(1, 8, arrived, 0)
    mycols = pl.multiple_of(k * 2048, 2048)
    matecols = pl.multiple_of((1 - k) * 2048, 2048)
    for i in range(4):
        n = slice(512 * i, 512 * i + 512)
        total = (dot(PT[...], RB[:, :, n].reshape(768, 512), NN) + BASE[:, n]).astype(HALF)
        XS[i] = total[128:256]
        send(XS.at[i], XR.at[i], xs.at[i], xr.at[i], part)
        tg[:, pl.ds(pl.multiple_of(mycols + 512 * i, 512), 512)] = total[0:128]

    for e in range(2):
        got(R2.at[e, 0], gs.at[e, 18], gr.at[e, 18])
        got(R2.at[e, 1], gs.at[e, 19], gr.at[e, 19])

        def final(i, _, e=e):
            r = pl.ds(pl.multiple_of(i * 32, 32), 32)
            total = ACC[e, r, :] + R2[e, 0, r, :].astype(SINGLE) + R2[e, 1, r, :].astype(SINGLE)
            kg[r, e, :] = total[:, 0:256]
            vg[r, e, :] = total[:, 256:512]
            return 0

        lax.fori_loop(0, 8, final, 0)
    for i in range(4):
        got(XR.at[i], xs.at[i], xr.at[i])
        tg[:, pl.ds(pl.multiple_of(matecols + 512 * i, 512), 512)] = XR[i]

    for d in pending:
        d.wait_send()
    drain(GB, gas, gar)
    drain(SD, ds, dr)
    drain(SS, ss, sr)
    drain(SW, vs, vr)
    drain(SM, ms, mr)
    drain_mem(MT, hs, hr)
    drain_mem(QGS, qs, qr)


def shards(tokens, picks, route_weight, cotangent, query_weight, key_weight, value_weight, gates):
    anywhere = pl.BlockSpec(memory_space=pl.ANY)
    vmem = pl.BlockSpec(memory_space=pltpu.VMEM)
    V = pltpu.VMEM
    S = pltpu.SemaphoreType.DMA
    tg, kg, vg = pl.pallas_call(
        kernel,
        out_shape=(
            jax.ShapeDtypeStruct((128, 4096), HALF),
            jax.ShapeDtypeStruct((256, 2, 256), SINGLE),
            jax.ShapeDtypeStruct((256, 2, 256), SINGLE),
        ),
        in_specs=[
            anywhere, vmem, vmem, anywhere, anywhere, vmem, vmem,
            pl.BlockSpec(memory_space=pltpu.SMEM),
        ],
        out_specs=(vmem, vmem, vmem),
        scratch_shapes=[
            V((8, 128, 4096), HALF),
            V((8, 128, 512), HALF),
            V((8, 8, 128), SINGLE),
            V((2, 16, 256, 512), HALF),
            V((4096, 256), HALF),
            V((2, 4, 48, 4096), HALF),
            V((4, 128, 256), HALF),
            V((2, 4, 48, 256), HALF),
            V((2, 16, 256, 512), HALF),
            V((2, 4, 2, 128, 512), HALF),
            V((2, 4, 2, 256, 512), HALF),
            V((2, 2, 128, 512), HALF),
            V((2, 2, 256, 512), HALF),
            V((2, 256, 512), SINGLE),
            V((2, 4, 96, 2048), HALF),
            V((8, 96, 2048), HALF),
            V((4, 128, 512), HALF),
            V((4, 128, 512), HALF),
            V((256, 768), HALF),
            V((4, 96, 256), HALF),
            V((8, 96, 256), HALF),
            V((256, 2048), SINGLE),
            V((2, 192, 512), SINGLE),
            V((16, 8, 256), SINGLE),
        ]
        + [V((16, 32, 256), HALF)] * 8
        + [
            V((2, 4, 48, 256), HALF),
            V((2, 192, 512), HALF),
            V((2, 192, 512), HALF),
            S((3,)),
            S((2, 20)), S((2, 20)),
            S((11,)), S((11,)),
            S((11,)), S((11,)),
            S((8,)), S((8,)),
            S((16,)), S((16,)),
            S((16,)), S((16,)),
            S((16,)), S((16,)),
            S((16,)), S((16,)),
            S((16,)), S((16,)),
            S((2, 20)), S((2, 20)),
            S((8,)), S((8,)),
            S((8,)), S((8,)),
            S((4,)), S((4,)),
        ],
        compiler_params=pltpu.CompilerParams(
            collective_id=0, has_side_effects=True, vmem_limit_bytes=60 * 1024 * 1024
        ),
    )(
        tokens, picks.T, route_weight.T, cotangent, query_weight, key_weight, value_weight,
        gates.transpose(0, 2, 1).reshape(2, 3),
    )
    return tg, kg, vg


def solution(mesh):
    return jax.shard_map(
        shards,
        mesh=mesh,
        in_specs=(
            P(("ctx", "mem"), None),
            P(("ctx", "mem"), None),
            P(("ctx", "mem"), None),
            P(("ctx", "mem"), None),
            P(),
            P("ctx", "mem", None),
            P("ctx", "mem", None),
            P("ctx", None, "mem"),
        ),
        out_specs=(P(("ctx", "mem"), None), P("ctx", "mem", None), P("ctx", "mem", None)),
        check_vma=False,
    )
```

```python
import jax
import jax.numpy as jnp
from jax import lax
from jax.experimental import pallas as pl
from jax.experimental.pallas import tpu as pltpu
from jax.sharding import PartitionSpec as P

MESH = pl.DeviceIdType.MESH
HALF = jnp.bfloat16
SINGLE = jnp.float32
TN = (((0,), (0,)), ((), ()))
NT = (((1,), (1,)), ((), ()))
NN = (((1,), (0,)), ((), ()))
OFFS_OUT = (0, 3, 1, 2)
OFFS_IN = (2, 1, 3, 0)


def dot(a, b, dims):
    return lax.dot_general(a, b, dims, preferred_element_type=SINGLE)


def kernel(
    tok, picks, weight, cot, qw, kw, vw, gates,
    tg, kg, vg,
    T, SIDE, MT, W, QW, OWN, SELT, QS, OS, GRS, G, F2, R2, ACC, CS, RB, XS, XR, PT, QGS, QGR, BASE, KVA,
    GB, SD, RD, SS, RSS, SW, RW, SM, RM, WT, KV,
    lsem, ws, wr, zs, zr, es, er, hs, hr, gas, gar, ds, dr, ss, sr, vs, vr, ms, mr, os_, or_, gs, gr, bs, br, qs, qr, xs, xr,
):
    c = lax.axis_index("ctx")
    m = lax.axis_index("mem")
    y, x = c // 4, c % 4
    z, k = m // 2, m % 2
    mate = m + 1 - 2 * k

    def mm(o, core):
        return ((z + o) % 4) * 2 + core

    pos = ((x, y), (y, x))

    def idx(e, p, s):
        return (s % 4) * 4 + p % 4 if e == 0 else (p % 4) * 4 + s % 4

    def to(e, dp, dsec):
        p, s = pos[e]
        return (idx(e, p + dp, s + dsec), m)

    def rc(src, dst, ssem, rsem, dev):
        return pltpu.make_async_remote_copy(
            src_ref=src, dst_ref=dst, send_sem=ssem, recv_sem=rsem,
            device_id=dev, device_id_type=MESH,
        )

    pending = []

    def send(src, dst, ssem, rsem, dev):
        d = rc(src, dst, ssem, rsem, dev)
        d.start()
        pending.append(d)

    def got(ref, ssem, rsem):
        rc(ref, ref, ssem, rsem, (c, mate)).wait_recv()

    locals_ = [
        pltpu.make_async_copy(tok, T.at[m], lsem.at[0]),
        pltpu.make_async_copy(qw, QW, lsem.at[1]),
        pltpu.make_async_copy(cot, SIDE.at[m, :, pl.ds(0, 256)], lsem.at[2]),
    ]
    for d in locals_:
        d.start()

    barrier = pltpu.get_barrier_semaphore()

    def greet(off, _):
        pl.semaphore_signal(barrier, inc=1, device_id=((c + off) % 16, m), device_id_type=MESH)
        return 0

    def greet_mem(off, _):
        pl.semaphore_signal(barrier, inc=1, device_id=(c, (m + off) % 8), device_id_type=MESH)
        return 0

    lax.fori_loop(1, 16, greet, 0)
    lax.fori_loop(1, 8, greet_mem, 0)
    for e in range(2):
        W[e, c, :, 0:256] = kw[:, e, :]
        W[e, c, :, 256:512] = vw[:, e, :]
        for g in range(3):
            GB[c, 2 * g + e:2 * g + e + 1, :] = jnp.full((1, 256), gates[e, g], SINGLE)
    GB[c, 6:8, :] = jnp.zeros((2, 256), SINGLE)
    MT[m] = jnp.concatenate(
        [picks[...].astype(SINGLE), weight[...].astype(SINGLE), jnp.zeros((4, 128), SINGLE)], axis=0
    )
    pl.semaphore_wait(barrier, 22)

    TOP, BOT = pl.ds(0, 64), pl.ds(64, 64)
    up, down, part = (c, mm(1, k)), (c, mm(3, k)), (c, mate)

    def zsend(buf, sems, slot, rows, n, dev):
        r = buf.at[slot] if rows is None else buf.at[slot, rows]
        send(r, r, sems[0].at[n], sems[1].at[n], dev)

    def zgot(buf, sems, slot, rows, n):
        got(buf.at[slot] if rows is None else buf.at[slot, rows], sems[0].at[n], sems[1].at[n])

    tz, ez = (zs, zr), (es, er)

    def z_start(buf, sems):
        zsend(buf, sems, m, TOP, 0, up)
        zsend(buf, sems, m, BOT, 1, down)
        zsend(buf, sems, m, BOT, 2, up)
        zsend(buf, sems, m, TOP, 3, down)
        zsend(buf, sems, m, None, 6, part)

    def z_forward(buf, sems):
        zgot(buf, sems, mm(3, k), TOP, 0)
        zsend(buf, sems, mm(3, k), TOP, 4, up)
        zgot(buf, sems, mm(1, k), BOT, 1)
        zsend(buf, sems, mm(1, k), BOT, 5, down)

    def z_hand(buf, sems):
        zgot(buf, sems, mm(3, k), BOT, 2)
        zsend(buf, sems, mm(3, k), None, 7, part)
        zgot(buf, sems, mm(1, k), TOP, 3)
        zsend(buf, sems, mm(1, k), None, 8, part)

    def z_far(buf, sems):
        zgot(buf, sems, mm(2, k), TOP, 4)
        zsend(buf, sems, mm(2, k), TOP, 9, part)
        zgot(buf, sems, mm(2, k), BOT, 5)
        zsend(buf, sems, mm(2, k), BOT, 10, part)

    def z_mate(buf, sems, o):
        if o == 2:
            zgot(buf, sems, mm(2, 1 - k), TOP, 9)
            zgot(buf, sems, mm(2, 1 - k), BOT, 10)
        else:
            zgot(buf, sems, mm(o, 1 - k), None, {0: 6, 3: 7, 1: 8}[o])

    HT, HB = pl.ds(0, 128), pl.ds(128, 128)

    def wsend(e, block, rows, n, dp, dsec):
        r = W.at[e, block] if rows is None else W.at[e, block, rows]
        send(r, r, ws.at[e, n], wr.at[e, n], to(e, dp, dsec))

    def wgot(e, block, rows, n):
        got(W.at[e, block] if rows is None else W.at[e, block, rows], ws.at[e, n], wr.at[e, n])

    def send_gate(off, _):
        there = (c + off) % 16
        rc(GB.at[c], GB.at[c], gas.at[off], gar.at[off], (there, m)).start()
        return 0

    def send_meta(off, _):
        there = (m + off) % 8
        rc(MT.at[m], MT.at[m], hs.at[off], hr.at[off], (c, there)).start()
        return 0

    lax.fori_loop(1, 8, send_meta, 0)
    lax.fori_loop(1, 16, send_gate, 0)
    for e in range(2):
        wsend(e, c, None, 0, 1, 0)
        wsend(e, c, None, 1, 3, 0)
    for e in range(2):
        wsend(e, c, None, 4, 0, 1)
        wsend(e, c, None, 5, 0, 3)
    for d in locals_:
        d.wait()
    SIDE[m, :, 256:512] = dot(T[m], QW[...], NN).astype(HALF)
    zsend(SIDE, ez, m, None, 2, (c, mm(2, k)))
    zsend(SIDE, ez, m, None, 0, up)
    zsend(SIDE, ez, m, None, 1, down)
    zsend(SIDE, ez, m, None, 6, part)
    z_start(T, tz)

    def side_hand(o):
        n = {3: 0, 1: 1, 2: 2}[o]
        zgot(SIDE, ez, mm(o, k), None, n)
        zsend(SIDE, ez, mm(o, k), None, 7 + n, part)

    def side_mate(o):
        zgot(SIDE, ez, mm(o, 1 - k), None, {0: 6, 3: 7, 1: 8, 2: 9}[o])

    def w_first(e):
        p, s = pos[e]
        b = idx(e, p + 3, s)
        wgot(e, b, None, 0)
        wsend(e, b, HT, 2, 1, 0)
        b = idx(e, p + 1, s)
        wgot(e, b, None, 1)
        wsend(e, b, HB, 3, 3, 0)

    def w_spread(e, i):
        p, s = pos[e]
        b = idx(e, p + OFFS_OUT[i], s)
        wsend(e, b, None, 4 + 4 * i, 0, 1)
        wsend(e, b, None, 5 + 4 * i, 0, 3)

    def w_far(e):
        p, s = pos[e]
        b = idx(e, p + 2, s)
        wgot(e, b, HT, 2)
        wgot(e, b, HB, 3)

    def w_second(e, i):
        p, s = pos[e]
        b = idx(e, p + OFFS_OUT[i], s + 3)
        wgot(e, b, None, 4 + 4 * i)
        wsend(e, b, HT, 6 + 4 * i, 0, 1)
        b = idx(e, p + OFFS_OUT[i], s + 1)
        wgot(e, b, None, 5 + 4 * i)
        wsend(e, b, HB, 7 + 4 * i, 0, 3)

    def w_last(e, i):
        p, s = pos[e]
        b = idx(e, p + OFFS_OUT[i], s + 2)
        wgot(e, b, HT, 6 + 4 * i)
        wgot(e, b, HB, 7 + 4 * i)

    sub = lax.broadcasted_iota(jnp.int32, (128, 128), 0)
    lane = lax.broadcasted_iota(jnp.int32, (128, 128), 1)
    before = jnp.where(sub < lane, 1.0, 0.0).astype(HALF)
    subf = sub.astype(SINGLE)
    mf = m.astype(SINGLE)

    def positions(d, core):
        meta = MT[d]
        p0, p1 = meta[0:1], meta[1:2]
        hits = jnp.where((subf == p0) | (subf == p1), 1.0, 0.0).astype(HALF)
        rank = dot(hits, before, NN)
        out = []
        for pk in (p0, p1):
            r = jnp.sum(jnp.where(subf == pk, rank, 0.0), axis=0, keepdims=True)
            out.append(48.0 * pk + 24.0 * core + r)
        return out

    def gather_side(o):
        zz = (z + o) % 4
        ws_, sels = [], []
        for core in range(2):
            p0, p1 = positions(2 * zz + core, float(core))
            at = subf + 96.0 * mf
            sel = jnp.where(((at == p0) | (at == p1)) & (sub < 96), 1.0, 0.0)
            meta = MT[2 * zz + core]
            w = []
            for e in range(2):
                pick = jnp.where(meta[0:1] == 2.0 * mf + e, meta[2:3], meta[3:4])
                w.append(jnp.sum(sel[48 * e:48 * e + 48] * pick, axis=1, keepdims=True))
            ws_.append(w)
            sels.append(sel.astype(HALF))
        sel = jnp.concatenate(sels, axis=1)
        SELT[zz] = sel
        got_side = dot(sel, SIDE[pl.ds(2 * zz, 2)].reshape(256, 512), NN)
        for e in range(2):
            w = ws_[0][e] + ws_[1][e]
            rows = got_side[48 * e:48 * e + 48]
            WT[e, zz] = (w * rows[:, 0:256]).astype(HALF)
            QS[e, zz] = rows[:, 256:512].astype(HALF)

    def gather(o):
        zz = (z + o) % 4
        for a in range(0, 4096, 1024):
            picked = dot(SELT[zz], T[pl.ds(2 * zz, 2), :, a:a + 1024].reshape(256, 1024), NN).astype(HALF)
            OWN[0, zz, :, a:a + 1024] = picked[0:48]
            for j in range(4):
                q = 1024 * j + a // 4
                OWN[1, zz, :, q:q + 256] = picked[48:96, 256 * j:256 * j + 256]

    def exchange(src, dst, ssem, rsem):
        def one(off, _):
            there = (c + off) % 16
            rc(src.at[there], dst.at[c], ssem.at[off], rsem.at[off], (there, m)).start()
            return 0

        lax.fori_loop(1, 16, one, 0)
        dst[c] = src[c]

    def collect(dst, ssem, rsem):
        def one(off, _):
            rc(dst.at[0], dst.at[(c - off + 16) % 16], ssem.at[off], rsem.at[off], (c, mate)).wait_recv()
            return 0

        lax.fori_loop(1, 16, one, 0)

    def drain(src, ssem, rsem):
        def one(off, _):
            rc(src.at[0], src.at[0], ssem.at[off], rsem.at[off], (c, mate)).wait_send()
            return 0

        lax.fori_loop(1, 16, one, 0)

    def collect_mem(dst, ssem, rsem):
        def one(off, _):
            rc(dst.at[0], dst.at[(m - off + 8) % 8], ssem.at[off], rsem.at[off], (c, mate)).wait_recv()
            return 0

        lax.fori_loop(1, 8, one, 0)

    def drain_mem(src, ssem, rsem):
        def one(off, _):
            rc(src.at[0], src.at[0], ssem.at[off], rsem.at[off], (c, mate)).wait_send()
            return 0

        lax.fori_loop(1, 8, one, 0)

    def gate(at, which):
        g = GB[at]
        return jnp.concatenate(
            [jnp.broadcast_to(g[2 * which + e:2 * which + e + 1], (16, 256)) for e in range(2)], axis=0
        )

    def kv_part(e, i):
        p, s = pos[e]
        total = KVA[e] if i else jnp.zeros((192, 512), SINGLE)
        for o in range(4):
            b = idx(e, p + OFFS_OUT[i], s + o)
            q = (s + o) % 4 * 4 + (p + OFFS_OUT[i]) % 4
            cols = OWN[e, :, :, pl.ds(pl.multiple_of(q * 256, 256), 256)].reshape(192, 256)
            total = total + dot(cols, W[e, b], NN)
        if i < 3:
            KVA[e] = total
        else:
            KV[e] = total.astype(HALF)

    def back(i, carry):
        at = 15 - i
        ct, ca = carry
        total = RD[at].astype(SINGLE) + ct
        adj = total + ca
        SS[at] = (gate(at, 2) * adj).astype(HALF)
        return gate(at, 1) * total, gate(at, 0) * adj

    zero = jnp.zeros((32, 256), SINGLE)
    w_first(0)
    w_first(1)
    for o in (3, 1, 2):
        side_hand(o)
    collect_mem(MT, hs, hr)
    for o in (0, 3, 1, 2):
        side_mate(o)
        gather_side(o)
    for e in range(2):
        direct = dot(WT[e].reshape(192, 256), QS[e].reshape(192, 256), TN).astype(HALF)
        SD[:, 16 * e:16 * e + 16, :] = direct.reshape(16, 16, 256)
    exchange(SD, RD, ds, dr)
    w_spread(0, 1)
    w_spread(1, 1)
    z_mate(T, tz, 0)
    gather(0)
    w_far(0)
    w_far(1)
    collect(GB, gas, gar)
    collect(RD, ds, dr)
    lax.fori_loop(0, 16, back, (zero, zero))
    exchange(SS, RSS, ss, sr)
    for i in (2, 3):
        for e in range(2):
            w_spread(e, i)
    z_forward(T, tz)
    w_second(0, 0)
    w_second(1, 0)
    rows768 = lax.broadcasted_iota(jnp.int32, (768, 128), 0).astype(SINGLE)
    kf = k.astype(SINGLE)
    for half, (d, core) in enumerate(((m, kf), (mate, 1.0 - kf))):
        p0, p1 = positions(d, core)
        hot = jnp.where((rows768 == p0) | (rows768 == p1), 1.0, 0.0)
        PT[128 * half:128 * half + 128, :] = hot.T.astype(HALF)
    w_second(0, 1)
    w_second(1, 1)
    w_second(0, 2)
    w_second(1, 2)
    z_hand(T, tz)
    z_mate(T, tz, 3)
    gather(3)
    w_second(0, 3)
    w_second(1, 3)
    z_mate(T, tz, 1)
    gather(1)
    collect(RSS, ss, sr)
    z_far(T, tz)
    z_mate(T, tz, 2)
    gather(2)

    def slices(e, o):
        p, s = pos[e]
        cols = pl.ds(pl.multiple_of((s + o) % 4 * 1024, 1024), 1024)
        send(OWN.at[e, :, :, cols], OS.at[e, s], os_.at[e, o], or_.at[e, o], to(e, 0, o))

    keep = []
    for e in range(2):
        slices(e, 2)
        s = pos[e][1]
        own = OWN.at[e, :, :, pl.ds(pl.multiple_of(s * 1024, 1024), 1024)]
        keep.append(pltpu.make_async_copy(own, OS.at[e, s], lsem.at[e]))
        keep[e].start()

    for i in range(4):
        for e in range(2):
            w_last(e, i)
            kv_part(e, i)
    for e in range(2):
        written = dot(KV[e, :, 256:512], KV[e, :, 0:256], TN)
        written = GB[c, 4 + e:5 + e, :] * written
        SW[:, 16 * e:16 * e + 16, :] = written.astype(HALF).reshape(16, 16, 256)
    exchange(SW, RW, vs, vr)
    for e in range(2):
        scaled = RSS[:, 16 * e:16 * e + 16, :].reshape(256, 256)
        s = pos[e][1]
        GRS[e, s, :, 0:256] = dot(KV[e, :, 256:512], scaled, NN).astype(HALF)
        GRS[e, s, :, 256:512] = dot(KV[e, :, 0:256], scaled, NT).astype(HALF)
        for o in (2, 1, 3):
            send(GRS.at[e, s], GRS.at[e, s], os_.at[e, 4 + o], or_.at[e, 4 + o], to(e, 0, o))

    def gsend(src, dst, e, n, dp):
        send(src, dst, gs.at[e, n], gr.at[e, n], to(e, dp, 0))

    def s_wait(e):
        s = pos[e][1]
        keep[e].wait()
        for o in (2, 1, 3):
            got(OS.at[e, (s - o + 4) % 4], os_.at[e, o], or_.at[e, o])
            got(GRS.at[e, (s - o + 4) % 4], os_.at[e, 4 + o], or_.at[e, 4 + o])

    def share(e, i):
        block = (pos[e][0] + OFFS_IN[i]) % 4
        cols = OS[e, :, :, :, pl.ds(pl.multiple_of(block * 256, 256), 256)].reshape(768, 256)
        total = dot(cols, GRS[e].reshape(768, 512), TN)
        if i == 3:
            ACC[e] = total
        else:
            G[e, i] = total.astype(HALF)
        if i == 0:
            gsend(G.at[e, 0, HT], F2.at[e, 0], e, 0, 1)
            gsend(G.at[e, 0, HB], F2.at[e, 1], e, 1, 3)

    def forth(at, carry):
        state, memory = carry
        state = gate(at, 0) * state + RW[at].astype(SINGLE)
        memory = gate(at, 1) * memory + state
        SM[at] = memory.astype(HALF)
        return state, memory

    def add_rows(dst, parts, start, rows, out=None):
        def one(i, _):
            r = pl.ds(pl.multiple_of(start + i * 32, 32), 32)
            total = dst[r, :].astype(SINGLE)
            for ref, base in parts:
                total = total + ref[pl.ds(pl.multiple_of(base + i * 32, 32), 32), :].astype(SINGLE)
            if out is None:
                dst[r, :] = total.astype(HALF)
            else:
                out[r, :] = total
            return 0

        lax.fori_loop(0, rows // 32, one, 0)

    def r_pass(e, i):
        got(F2.at[e, i - 1], gs.at[e, i - 1], gr.at[e, i - 1])
        add_rows(G.at[e, i], [(F2.at[e, i - 1], 0)], 128 * (i - 1), 128)
        gsend(G.at[e, i], R2.at[e, i - 1], e, 1 + i, 1 if i == 1 else 3)

    def bsend(src, dst, n, part_, slot, dev):
        send(src, dst, bs.at[part_, n], br.at[part_, slot], (c, dev))

    def contribute(h, half):
        def column(i, _):
            for e in range(2):
                out = dot(GRS[e, pos[e][1]], W[e, 8 * h + i], NT)
                CS[h, :, 48 * e:48 * e + 48, pl.ds(pl.multiple_of(i * 256, 256), 256)] = (
                    out.astype(HALF).reshape(4, 48, 256)
                )
            return 0

        lax.fori_loop(4 * half, 4 * half + 4, column, 0)

    def dispatch(h, half, chips):
        cols = pl.ds(1024 * half, 1024)
        for o in chips:
            bsend(CS.at[h, (z + o) % 4, :, cols], RB.at[m, :, cols], 4 * h + o, half, m, mm(o, h))

    contribute(0, 0)
    dispatch(0, 0, (2, 1, 3))
    contribute(0, 1)
    dispatch(0, 1, (2, 1, 3))
    collect(RW, vs, vr)
    lax.fori_loop(0, 16, forth, (zero, zero))
    exchange(SM, RM, ms, mr)
    for o in (1, 3):
        for e in range(2):
            slices(e, o)
    contribute(1, 0)
    dispatch(1, 0, (2, 1, 3))
    contribute(1, 1)
    dispatch(1, 1, (2,))

    collect(RM, ms, mr)
    for e in range(2):
        memory = RM[:, 16 * e:16 * e + 16, :].reshape(256, 256)
        grad = dot(WT[e].reshape(192, 256), memory, NN).astype(HALF)
        QGS[:, 48 * e:48 * e + 48, :] = grad.reshape(4, 48, 256)

    def send_query(off, _):
        there = (m + off) % 8
        rc(QGS.at[there // 2], QGR.at[m], qs.at[off], qr.at[off], (c, there)).start()
        return 0

    lax.fori_loop(1, 8, send_query, 0)
    QGR[m] = QGS[z]
    dispatch(1, 1, (1, 3))
    for half in range(2):
        cols = pl.ds(1024 * half, 1024)
        bsend(CS.at[1 - k, z, :, cols], RB.at[m, :, cols], 0, half, m, mate)
    RB[m] = CS[k, z]
    for e in range(2):
        s_wait(e)
        for i in range(3):
            share(e, i)
    for e in range(2):
        r_pass(e, 1)
        r_pass(e, 2)
        share(e, 3)
    collect_mem(QGR, qs, qr)
    grads = dot(PT[...], QGR[...].reshape(768, 256), NN).astype(HALF)

    def base(i, _):
        n = pl.multiple_of(i * 512, 512)
        BASE[:, pl.ds(n, 512)] = dot(grads, QW[pl.ds(pl.multiple_of(k * 2048 + n, 512), 512), :], NT)
        return 0

    lax.fori_loop(0, 4, base, 0)

    mycols = pl.multiple_of(k * 2048, 2048)
    matecols = pl.multiple_of((1 - k) * 2048, 2048)
    for half in range(2):
        def arrived(off, _):
            there = (m + off) % 8
            cols = pl.ds(1024 * half, 1024)
            rc(RB.at[0, :, cols], RB.at[there, :, cols], bs.at[half, 0], br.at[half, there], (c, mate)).wait_recv()
            return 0

        lax.fori_loop(1, 8, arrived, 0)
        for i in (2 * half, 2 * half + 1):
            n = slice(512 * i, 512 * i + 512)
            total = (dot(PT[...], RB[:, :, n].reshape(768, 512), NN) + BASE[:, n]).astype(HALF)
            XS[i] = total[128:256]
            send(XS.at[i], XR.at[i], xs.at[i], xr.at[i], part)
            tg[:, pl.ds(pl.multiple_of(mycols + 512 * i, 512), 512)] = total[0:128]

    for e in range(2):
        got(R2.at[e, 0], gs.at[e, 2], gr.at[e, 2])
        got(R2.at[e, 1], gs.at[e, 3], gr.at[e, 3])

        def final(i, _, e=e):
            r = pl.ds(pl.multiple_of(i * 32, 32), 32)
            total = ACC[e, r, :] + R2[e, 0, r, :].astype(SINGLE) + R2[e, 1, r, :].astype(SINGLE)
            kg[r, e, :] = total[:, 0:256]
            vg[r, e, :] = total[:, 256:512]
            return 0

        lax.fori_loop(0, 8, final, 0)
    for i in range(4):
        got(XR.at[i], xs.at[i], xr.at[i])
        tg[:, pl.ds(pl.multiple_of(matecols + 512 * i, 512), 512)] = XR[i]

    for d in pending:
        d.wait_send()
    drain(GB, gas, gar)
    drain(SD, ds, dr)
    drain(SS, ss, sr)
    drain(SW, vs, vr)
    drain(SM, ms, mr)
    drain_mem(MT, hs, hr)
    drain_mem(QGS, qs, qr)


def shards(tokens, picks, route_weight, cotangent, query_weight, key_weight, value_weight, gates):
    anywhere = pl.BlockSpec(memory_space=pl.ANY)
    vmem = pl.BlockSpec(memory_space=pltpu.VMEM)
    V = pltpu.VMEM
    S = pltpu.SemaphoreType.DMA
    tg, kg, vg = pl.pallas_call(
        kernel,
        out_shape=(
            jax.ShapeDtypeStruct((128, 4096), HALF),
            jax.ShapeDtypeStruct((256, 2, 256), SINGLE),
            jax.ShapeDtypeStruct((256, 2, 256), SINGLE),
        ),
        in_specs=[
            anywhere, vmem, vmem, anywhere, anywhere, vmem, vmem,
            pl.BlockSpec(memory_space=pltpu.SMEM),
        ],
        out_specs=(vmem, vmem, vmem),
        scratch_shapes=[
            V((8, 128, 4096), HALF),
            V((8, 128, 512), HALF),
            V((8, 8, 128), SINGLE),
            V((2, 16, 256, 512), HALF),
            V((4096, 256), HALF),
            V((2, 4, 48, 4096), HALF),
            V((4, 128, 256), HALF),
            V((2, 4, 48, 256), HALF),
            V((2, 4, 4, 48, 1024), HALF),
            V((2, 4, 192, 512), HALF),
            V((2, 3, 256, 512), HALF),
            V((2, 2, 128, 512), HALF),
            V((2, 2, 256, 512), HALF),
            V((2, 256, 512), SINGLE),
            V((2, 4, 96, 2048), HALF),
            V((8, 96, 2048), HALF),
            V((4, 128, 512), HALF),
            V((4, 128, 512), HALF),
            V((256, 768), HALF),
            V((4, 96, 256), HALF),
            V((8, 96, 256), HALF),
            V((256, 2048), SINGLE),
            V((2, 192, 512), SINGLE),
            V((16, 8, 256), SINGLE),
        ]
        + [V((16, 32, 256), HALF)] * 8
        + [
            V((2, 4, 48, 256), HALF),
            V((2, 192, 512), HALF),
            S((3,)),
            S((2, 20)), S((2, 20)),
            S((11,)), S((11,)),
            S((11,)), S((11,)),
            S((8,)), S((8,)),
            S((16,)), S((16,)),
            S((16,)), S((16,)),
            S((16,)), S((16,)),
            S((16,)), S((16,)),
            S((16,)), S((16,)),
            S((2, 8)), S((2, 8)),
            S((2, 4)), S((2, 4)),
            S((2, 8)), S((2, 8)),
            S((8,)), S((8,)),
            S((4,)), S((4,)),
        ],
        compiler_params=pltpu.CompilerParams(
            collective_id=0, has_side_effects=True, vmem_limit_bytes=60 * 1024 * 1024
        ),
    )(
        tokens, picks.T, route_weight.T, cotangent, query_weight, key_weight, value_weight,
        gates.transpose(0, 2, 1).reshape(2, 3),
    )
    return tg, kg, vg


def solution(mesh):
    return jax.shard_map(
        shards,
        mesh=mesh,
        in_specs=(
            P(("ctx", "mem"), None),
            P(("ctx", "mem"), None),
            P(("ctx", "mem"), None),
            P(("ctx", "mem"), None),
            P(),
            P("ctx", "mem", None),
            P("ctx", "mem", None),
            P("ctx", None, "mem"),
        ),
        out_specs=(P(("ctx", "mem"), None), P("ctx", "mem", None), P("ctx", "mem", None)),
        check_vma=False,
    )
```

```python
import jax
import jax.numpy as jnp
from jax import lax
from jax.experimental import pallas as pl
from jax.experimental.pallas import tpu as pltpu
from jax.sharding import PartitionSpec as P

MESH = pl.DeviceIdType.MESH
HALF = jnp.bfloat16
SINGLE = jnp.float32
TN = (((0,), (0,)), ((), ()))
NT = (((1,), (1,)), ((), ()))
NN = (((1,), (0,)), ((), ()))
OFFS_OUT = (0, 3, 1, 2)
OFFS_IN = (2, 1, 3, 0)


def dot(a, b, dims):
    return lax.dot_general(a, b, dims, preferred_element_type=SINGLE)


def kernel(
    tok, picks, weight, cot, qw, kw_any, vw_any, gates,
    tg_any, kg_any, vg_any,
    kw, vw, tg, kg, vg,
    T, SIDE, MT, W, QW, OWN, SELT, QS, OS, GRS, G, F2, R2, ACC, CS, RB, XS, XR, PT, QGS, QGR, BASE, KVA,
    GB, SD, RD, SS, RSS, SW, RW, SM, RM, WT, KV,
    lsem, ws, wr, zs, zr, es, er, hs, hr, gas, gar, ds, dr, ss, sr, vs, vr, ms, mr, os_, or_, gs, gr, bs, br, qs, qr, xs, xr,
):
    c = lax.axis_index("ctx")
    m = lax.axis_index("mem")
    y, x = c // 4, c % 4
    z, k = m // 2, m % 2
    mate = m + 1 - 2 * k

    def mm(o, core):
        return ((z + o) % 4) * 2 + core

    pos = ((x, y), (y, x))

    def idx(e, p, s):
        return (s % 4) * 4 + p % 4 if e == 0 else (p % 4) * 4 + s % 4

    def to(e, dp, dsec):
        p, s = pos[e]
        return (idx(e, p + dp, s + dsec), m)

    def rc(src, dst, ssem, rsem, dev):
        return pltpu.make_async_remote_copy(
            src_ref=src, dst_ref=dst, send_sem=ssem, recv_sem=rsem,
            device_id=dev, device_id_type=MESH,
        )

    pending = []

    def send(src, dst, ssem, rsem, dev):
        d = rc(src, dst, ssem, rsem, dev)
        d.start()
        pending.append(d)

    def flush():
        for d in pending:
            d.wait_send()
        pending.clear()

    def got(ref, ssem, rsem):
        rc(ref, ref, ssem, rsem, (c, mate)).wait_recv()

    weights_ = [
        pltpu.make_async_copy(kw_any, kw, lsem.at[3]),
        pltpu.make_async_copy(vw_any, vw, lsem.at[4]),
    ]
    for d in weights_:
        d.start()
    locals_ = [
        pltpu.make_async_copy(tok, T.at[m], lsem.at[0]),
        pltpu.make_async_copy(qw, QW, lsem.at[1]),
        pltpu.make_async_copy(cot, SIDE.at[m, :, pl.ds(0, 256)], lsem.at[2]),
    ]
    for d in locals_:
        d.start()

    barrier = pltpu.get_barrier_semaphore()

    def greet(off, _):
        pl.semaphore_signal(barrier, inc=1, device_id=((c + off) % 16, m), device_id_type=MESH)
        return 0

    def greet_mem(off, _):
        pl.semaphore_signal(barrier, inc=1, device_id=(c, (m + off) % 8), device_id_type=MESH)
        return 0

    lax.fori_loop(1, 16, greet, 0)
    lax.fori_loop(1, 8, greet_mem, 0)
    for d in weights_:
        d.wait()
    for e in range(2):
        W[e, c, :, 0:256] = kw[:, e, :]
        W[e, c, :, 256:512] = vw[:, e, :]
        for g in range(3):
            GB[c, 2 * g + e:2 * g + e + 1, :] = jnp.full((1, 256), gates[e, g], SINGLE)
    GB[c, 6:8, :] = jnp.zeros((2, 256), SINGLE)
    MT[m] = jnp.concatenate(
        [picks[...].astype(SINGLE), weight[...].astype(SINGLE), jnp.zeros((4, 128), SINGLE)], axis=0
    )
    pl.semaphore_wait(barrier, 22)

    TOP, BOT = pl.ds(0, 64), pl.ds(64, 64)
    up, down, part = (c, mm(1, k)), (c, mm(3, k)), (c, mate)

    def zsend(buf, sems, slot, rows, n, dev):
        r = buf.at[slot] if rows is None else buf.at[slot, rows]
        send(r, r, sems[0].at[n], sems[1].at[n], dev)

    def zgot(buf, sems, slot, rows, n):
        got(buf.at[slot] if rows is None else buf.at[slot, rows], sems[0].at[n], sems[1].at[n])

    tz, ez = (zs, zr), (es, er)

    def z_start(buf, sems):
        zsend(buf, sems, m, TOP, 0, up)
        zsend(buf, sems, m, BOT, 1, down)
        zsend(buf, sems, m, BOT, 2, up)
        zsend(buf, sems, m, TOP, 3, down)
        zsend(buf, sems, m, None, 6, part)

    def z_forward(buf, sems):
        zgot(buf, sems, mm(3, k), TOP, 0)
        zsend(buf, sems, mm(3, k), TOP, 4, up)
        zgot(buf, sems, mm(1, k), BOT, 1)
        zsend(buf, sems, mm(1, k), BOT, 5, down)

    def z_hand(buf, sems):
        zgot(buf, sems, mm(3, k), BOT, 2)
        zsend(buf, sems, mm(3, k), None, 7, part)
        zgot(buf, sems, mm(1, k), TOP, 3)
        zsend(buf, sems, mm(1, k), None, 8, part)

    def z_far(buf, sems):
        zgot(buf, sems, mm(2, k), TOP, 4)
        zsend(buf, sems, mm(2, k), TOP, 9, part)
        zgot(buf, sems, mm(2, k), BOT, 5)
        zsend(buf, sems, mm(2, k), BOT, 10, part)

    def z_mate(buf, sems, o):
        if o == 2:
            zgot(buf, sems, mm(2, 1 - k), TOP, 9)
            zgot(buf, sems, mm(2, 1 - k), BOT, 10)
        else:
            zgot(buf, sems, mm(o, 1 - k), None, {0: 6, 3: 7, 1: 8}[o])

    HT, HB = pl.ds(0, 128), pl.ds(128, 128)

    def wsend(e, block, rows, n, dp, dsec):
        r = W.at[e, block] if rows is None else W.at[e, block, rows]
        send(r, r, ws.at[e, n], wr.at[e, n], to(e, dp, dsec))

    def wgot(e, block, rows, n):
        got(W.at[e, block] if rows is None else W.at[e, block, rows], ws.at[e, n], wr.at[e, n])

    def send_gate(off, _):
        there = (c + off) % 16
        rc(GB.at[c], GB.at[c], gas.at[off], gar.at[off], (there, m)).start()
        return 0

    def send_meta(off, _):
        there = (m + off) % 8
        rc(MT.at[m], MT.at[m], hs.at[off], hr.at[off], (c, there)).start()
        return 0

    for e in range(2):
        wsend(e, c, None, 0, 1, 0)
        wsend(e, c, None, 1, 3, 0)
    for e in range(2):
        wsend(e, c, None, 4, 0, 1)
        wsend(e, c, None, 5, 0, 3)
    lax.fori_loop(1, 8, send_meta, 0)
    for d in locals_:
        d.wait()
    SIDE[m, :, 256:512] = dot(T[m], QW[...], NN).astype(HALF)
    zsend(SIDE, ez, m, None, 2, (c, mm(2, k)))
    zsend(SIDE, ez, m, None, 0, up)
    zsend(SIDE, ez, m, None, 1, down)
    zsend(SIDE, ez, m, None, 6, part)
    z_start(T, tz)
    lax.fori_loop(1, 16, send_gate, 0)

    def side_hand(o):
        n = {3: 0, 1: 1, 2: 2}[o]
        zgot(SIDE, ez, mm(o, k), None, n)
        zsend(SIDE, ez, mm(o, k), None, 7 + n, part)

    def side_mate(o):
        zgot(SIDE, ez, mm(o, 1 - k), None, {0: 6, 3: 7, 1: 8, 2: 9}[o])

    def w_first(e):
        p, s = pos[e]
        b = idx(e, p + 3, s)
        wgot(e, b, None, 0)
        wsend(e, b, HT, 2, 1, 0)
        b = idx(e, p + 1, s)
        wgot(e, b, None, 1)
        wsend(e, b, HB, 3, 3, 0)

    def w_spread(e, i):
        p, s = pos[e]
        b = idx(e, p + OFFS_OUT[i], s)
        wsend(e, b, None, 4 + 4 * i, 0, 1)
        wsend(e, b, None, 5 + 4 * i, 0, 3)

    def w_far(e):
        p, s = pos[e]
        b = idx(e, p + 2, s)
        wgot(e, b, HT, 2)
        wgot(e, b, HB, 3)

    def w_second(e, i):
        p, s = pos[e]
        b = idx(e, p + OFFS_OUT[i], s + 3)
        wgot(e, b, None, 4 + 4 * i)
        wsend(e, b, HT, 6 + 4 * i, 0, 1)
        b = idx(e, p + OFFS_OUT[i], s + 1)
        wgot(e, b, None, 5 + 4 * i)
        wsend(e, b, HB, 7 + 4 * i, 0, 3)

    def w_last(e, i):
        p, s = pos[e]
        b = idx(e, p + OFFS_OUT[i], s + 2)
        wgot(e, b, HT, 6 + 4 * i)
        wgot(e, b, HB, 7 + 4 * i)

    sub = lax.broadcasted_iota(jnp.int32, (128, 128), 0)
    lane = lax.broadcasted_iota(jnp.int32, (128, 128), 1)
    before = jnp.where(sub < lane, 1.0, 0.0).astype(HALF)
    subf = sub.astype(SINGLE)
    mf = m.astype(SINGLE)

    def positions(d, core):
        meta = MT[d]
        p0, p1 = meta[0:1], meta[1:2]
        hits = jnp.where((subf == p0) | (subf == p1), 1.0, 0.0).astype(HALF)
        rank = dot(hits, before, NN)
        out = []
        for pk in (p0, p1):
            r = jnp.sum(jnp.where(subf == pk, rank, 0.0), axis=0, keepdims=True)
            out.append(48.0 * pk + 24.0 * core + r)
        return out

    def gather_side(o):
        zz = (z + o) % 4
        ws_, sels = [], []
        for core in range(2):
            p0, p1 = positions(2 * zz + core, float(core))
            at = subf + 96.0 * mf
            sel = jnp.where(((at == p0) | (at == p1)) & (sub < 96), 1.0, 0.0)
            meta = MT[2 * zz + core]
            w = []
            for e in range(2):
                pick = jnp.where(meta[0:1] == 2.0 * mf + e, meta[2:3], meta[3:4])
                w.append(jnp.sum(sel[48 * e:48 * e + 48] * pick, axis=1, keepdims=True))
            ws_.append(w)
            sels.append(sel.astype(HALF))
        sel = jnp.concatenate(sels, axis=1)
        SELT[zz] = sel
        got_side = dot(sel, SIDE[pl.ds(2 * zz, 2)].reshape(256, 512), NN)
        for e in range(2):
            w = ws_[0][e] + ws_[1][e]
            rows = got_side[48 * e:48 * e + 48]
            WT[e, zz] = (w * rows[:, 0:256]).astype(HALF)
            QS[e, zz] = rows[:, 256:512].astype(HALF)

    def gather(o):
        zz = (z + o) % 4
        for a in range(0, 4096, 1024):
            picked = dot(SELT[zz], T[pl.ds(2 * zz, 2), :, a:a + 1024].reshape(256, 1024), NN).astype(HALF)
            OWN[0, zz, :, a:a + 1024] = picked[0:48]
            for j in range(4):
                q = 1024 * j + a // 4
                OWN[1, zz, :, q:q + 256] = picked[48:96, 256 * j:256 * j + 256]

    def exchange(src, dst, ssem, rsem):
        def one(off, _):
            there = (c + off) % 16
            rc(src.at[there], dst.at[c], ssem.at[off], rsem.at[off], (there, m)).start()
            return 0

        lax.fori_loop(1, 16, one, 0)
        dst[c] = src[c]

    def collect(dst, ssem, rsem):
        def one(off, _):
            rc(dst.at[0], dst.at[(c - off + 16) % 16], ssem.at[off], rsem.at[off], (c, mate)).wait_recv()
            return 0

        lax.fori_loop(1, 16, one, 0)

    def drain(src, ssem, rsem):
        def one(off, _):
            rc(src.at[0], src.at[0], ssem.at[off], rsem.at[off], (c, mate)).wait_send()
            return 0

        lax.fori_loop(1, 16, one, 0)

    def collect_mem(dst, ssem, rsem):
        def one(off, _):
            rc(dst.at[0], dst.at[(m - off + 8) % 8], ssem.at[off], rsem.at[off], (c, mate)).wait_recv()
            return 0

        lax.fori_loop(1, 8, one, 0)

    def drain_mem(src, ssem, rsem):
        def one(off, _):
            rc(src.at[0], src.at[0], ssem.at[off], rsem.at[off], (c, mate)).wait_send()
            return 0

        lax.fori_loop(1, 8, one, 0)

    def gate(at, which):
        g = GB[at]
        return jnp.concatenate(
            [jnp.broadcast_to(g[2 * which + e:2 * which + e + 1], (16, 256)) for e in range(2)], axis=0
        )

    def kv_part(e, i):
        p, s = pos[e]
        total = KVA[e] if i else jnp.zeros((192, 512), SINGLE)
        for o in range(4):
            b = idx(e, p + OFFS_OUT[i], s + o)
            q = (s + o) % 4 * 4 + (p + OFFS_OUT[i]) % 4
            cols = OWN[e, :, :, pl.ds(pl.multiple_of(q * 256, 256), 256)].reshape(192, 256)
            total = total + dot(cols, W[e, b], NN)
        if i < 3:
            KVA[e] = total
        else:
            KV[e] = total.astype(HALF)

    def back(i, carry):
        at = 15 - i
        ct, ca = carry
        total = RD[at].astype(SINGLE) + ct
        adj = total + ca
        SS[at] = (gate(at, 2) * adj).astype(HALF)
        return gate(at, 1) * total, gate(at, 0) * adj

    zero = jnp.zeros((32, 256), SINGLE)
    w_first(0)
    w_first(1)
    w_spread(0, 1)
    w_spread(1, 1)
    for o in (3, 1, 2):
        side_hand(o)
    collect_mem(MT, hs, hr)
    for o in (0, 3, 1, 2):
        side_mate(o)
        gather_side(o)
    for e in range(2):
        direct = dot(WT[e].reshape(192, 256), QS[e].reshape(192, 256), TN).astype(HALF)
        SD[:, 16 * e:16 * e + 16, :] = direct.reshape(16, 16, 256)
    exchange(SD, RD, ds, dr)
    w_spread(0, 2)
    w_spread(1, 2)
    z_mate(T, tz, 0)
    gather(0)
    w_far(0)
    w_far(1)
    w_spread(0, 3)
    w_spread(1, 3)
    w_second(0, 0)
    w_second(1, 0)
    z_forward(T, tz)
    rows768 = lax.broadcasted_iota(jnp.int32, (768, 128), 0).astype(SINGLE)
    kf = k.astype(SINGLE)
    for half, (d, core) in enumerate(((m, kf), (mate, 1.0 - kf))):
        p0, p1 = positions(d, core)
        hot = jnp.where((rows768 == p0) | (rows768 == p1), 1.0, 0.0)
        PT[128 * half:128 * half + 128, :] = hot.T.astype(HALF)
    collect(GB, gas, gar)
    collect(RD, ds, dr)
    lax.fori_loop(0, 16, back, (zero, zero))
    exchange(SS, RSS, ss, sr)
    w_second(0, 1)
    w_second(1, 1)
    w_second(0, 2)
    w_second(1, 2)
    z_hand(T, tz)
    z_mate(T, tz, 3)
    gather(3)
    w_second(0, 3)
    w_second(1, 3)
    z_mate(T, tz, 1)
    gather(1)
    collect(RSS, ss, sr)
    z_far(T, tz)
    z_mate(T, tz, 2)
    gather(2)

    early = list(pending)
    pending.clear()

    def slices(e, o):
        p, s = pos[e]
        cols = pl.ds(pl.multiple_of((s + o) % 4 * 1024, 1024), 1024)
        send(OWN.at[e, :, :, cols], OS.at[e, s], os_.at[e, o], or_.at[e, o], to(e, 0, o))

    keep = []
    for e in range(2):
        slices(e, 2)
        s = pos[e][1]
        own = OWN.at[e, :, :, pl.ds(pl.multiple_of(s * 1024, 1024), 1024)]
        keep.append(pltpu.make_async_copy(own, OS.at[e, s], lsem.at[e]))
        keep[e].start()

    for i in range(4):
        for e in range(2):
            w_last(e, i)
            kv_part(e, i)
    for e in range(2):
        written = dot(KV[e, :, 256:512], KV[e, :, 0:256], TN)
        written = GB[c, 4 + e:5 + e, :] * written
        SW[:, 16 * e:16 * e + 16, :] = written.astype(HALF).reshape(16, 16, 256)
    exchange(SW, RW, vs, vr)
    for e in range(2):
        scaled = RSS[:, 16 * e:16 * e + 16, :].reshape(256, 256)
        s = pos[e][1]
        GRS[e, s, :, 0:256] = dot(KV[e, :, 256:512], scaled, NN).astype(HALF)
        GRS[e, s, :, 256:512] = dot(KV[e, :, 0:256], scaled, NT).astype(HALF)
        for o in (1, 3):
            send(GRS.at[e, s], GRS.at[e, s], os_.at[e, 4 + o], or_.at[e, 4 + o], to(e, 0, o))

    def gsend(src, dst, e, n, dp):
        send(src, dst, gs.at[e, n], gr.at[e, n], to(e, dp, 0))

    def s_forward(e):
        s = pos[e][1]
        before_, after = (s + 3) % 4, (s + 1) % 4
        got(GRS.at[e, before_], os_.at[e, 5], or_.at[e, 5])
        ref = GRS.at[e, before_, pl.ds(0, 96)]
        send(ref, ref, os_.at[e, 6], or_.at[e, 6], to(e, 0, 1))
        got(GRS.at[e, after], os_.at[e, 7], or_.at[e, 7])
        ref = GRS.at[e, after, pl.ds(96, 96)]
        send(ref, ref, os_.at[e, 4], or_.at[e, 4], to(e, 0, 3))

    def s_wait(e):
        s = pos[e][1]
        keep[e].wait()
        got(GRS.at[e, (s + 2) % 4, pl.ds(0, 96)], os_.at[e, 6], or_.at[e, 6])
        got(GRS.at[e, (s + 2) % 4, pl.ds(96, 96)], os_.at[e, 4], or_.at[e, 4])
        for o in (2, 1, 3):
            got(OS.at[e, (s - o + 4) % 4], os_.at[e, o], or_.at[e, o])

    def share(e, i):
        block = (pos[e][0] + OFFS_IN[i]) % 4
        cols = OS[e, :, :, :, pl.ds(pl.multiple_of(block * 256, 256), 256)].reshape(768, 256)
        total = dot(cols, GRS[e].reshape(768, 512), TN)
        if i == 3:
            ACC[e] = total
        else:
            G[e, i] = total.astype(HALF)
        if i == 0:
            gsend(G.at[e, 0, HT], F2.at[e, 0], e, 0, 1)
            gsend(G.at[e, 0, HB], F2.at[e, 1], e, 1, 3)

    def forth(at, carry):
        state, memory = carry
        state = gate(at, 0) * state + RW[at].astype(SINGLE)
        memory = gate(at, 1) * memory + state
        SM[at] = memory.astype(HALF)
        return state, memory

    def add_rows(dst, parts, start, rows, out=None):
        def one(i, _):
            r = pl.ds(pl.multiple_of(start + i * 32, 32), 32)
            total = dst[r, :].astype(SINGLE)
            for ref, base in parts:
                total = total + ref[pl.ds(pl.multiple_of(base + i * 32, 32), 32), :].astype(SINGLE)
            if out is None:
                dst[r, :] = total.astype(HALF)
            else:
                out[r, :] = total
            return 0

        lax.fori_loop(0, rows // 32, one, 0)

    def r_pass(e, i):
        got(F2.at[e, i - 1], gs.at[e, i - 1], gr.at[e, i - 1])
        add_rows(G.at[e, i], [(F2.at[e, i - 1], 0)], 128 * (i - 1), 128)
        gsend(G.at[e, i], R2.at[e, i - 1], e, 1 + i, 1 if i == 1 else 3)

    def bsend(src, dst, n, part_, slot, dev):
        send(src, dst, bs.at[part_, n], br.at[part_, slot], (c, dev))

    def contribute(h, half):
        def column(i, _):
            for e in range(2):
                out = dot(GRS[e, pos[e][1]], W[e, 8 * h + i], NT)
                CS[h, :, 48 * e:48 * e + 48, pl.ds(pl.multiple_of(i * 256, 256), 256)] = (
                    out.astype(HALF).reshape(4, 48, 256)
                )
            return 0

        lax.fori_loop(4 * half, 4 * half + 4, column, 0)

    def dispatch(h, half, chips):
        cols = pl.ds(1024 * half, 1024)
        for o in chips:
            bsend(CS.at[h, (z + o) % 4, :, cols], RB.at[m, :, cols], 4 * h + o, half, m, mm(o, h))

    contribute(0, 0)
    dispatch(0, 0, (2, 1, 3))
    contribute(0, 1)
    dispatch(0, 1, (2, 1, 3))
    collect(RW, vs, vr)
    lax.fori_loop(0, 16, forth, (zero, zero))
    exchange(SM, RM, ms, mr)
    for o in (1, 3):
        for e in range(2):
            slices(e, o)
    contribute(1, 0)
    dispatch(1, 0, (2, 1, 3))
    s_forward(0)
    s_forward(1)
    contribute(1, 1)
    dispatch(1, 1, (2,))

    collect(RM, ms, mr)
    for e in range(2):
        memory = RM[:, 16 * e:16 * e + 16, :].reshape(256, 256)
        grad = dot(WT[e].reshape(192, 256), memory, NN).astype(HALF)
        QGS[:, 48 * e:48 * e + 48, :] = grad.reshape(4, 48, 256)

    def send_query(off, _):
        there = (m + off) % 8
        rc(QGS.at[there // 2], QGR.at[m], qs.at[off], qr.at[off], (c, there)).start()
        return 0

    lax.fori_loop(1, 8, send_query, 0)
    QGR[m] = QGS[z]
    dispatch(1, 1, (1, 3))
    for half in range(2):
        cols = pl.ds(1024 * half, 1024)
        bsend(CS.at[1 - k, z, :, cols], RB.at[m, :, cols], 0, half, m, mate)
    RB[m] = CS[k, z]
    for d in early:
        d.wait_send()
    drain(GB, gas, gar)
    drain(SD, ds, dr)
    drain(SS, ss, sr)
    drain(SW, vs, vr)
    drain(SM, ms, mr)
    drain_mem(MT, hs, hr)
    for e in range(2):
        s_wait(e)
        for i in range(3):
            share(e, i)
    for e in range(2):
        r_pass(e, 1)
        r_pass(e, 2)
        share(e, 3)
    collect_mem(QGR, qs, qr)
    grads = dot(PT[...], QGR[...].reshape(768, 256), NN).astype(HALF)

    def base(i, _):
        n = pl.multiple_of(i * 512, 512)
        BASE[:, pl.ds(n, 512)] = dot(grads, QW[pl.ds(pl.multiple_of(k * 2048 + n, 512), 512), :], NT)
        return 0

    lax.fori_loop(0, 4, base, 0)

    mycols = pl.multiple_of(k * 2048, 2048)
    matecols = pl.multiple_of((1 - k) * 2048, 2048)
    for half in range(2):
        def arrived(off, _):
            there = (m + off) % 8
            cols = pl.ds(1024 * half, 1024)
            rc(RB.at[0, :, cols], RB.at[there, :, cols], bs.at[half, 0], br.at[half, there], (c, mate)).wait_recv()
            return 0

        lax.fori_loop(1, 8, arrived, 0)
        for i in (2 * half, 2 * half + 1):
            n = slice(512 * i, 512 * i + 512)
            total = (dot(PT[...], RB[:, :, n].reshape(768, 512), NN) + BASE[:, n]).astype(HALF)
            XS[i] = total[128:256]
            send(XS.at[i], XR.at[i], xs.at[i], xr.at[i], part)
            tg[:, pl.ds(pl.multiple_of(mycols + 512 * i, 512), 512)] = total[0:128]

    for e in range(2):
        got(R2.at[e, 0], gs.at[e, 2], gr.at[e, 2])
        got(R2.at[e, 1], gs.at[e, 3], gr.at[e, 3])

        def final(i, _, e=e):
            r = pl.ds(pl.multiple_of(i * 32, 32), 32)
            total = ACC[e, r, :] + R2[e, 0, r, :].astype(SINGLE) + R2[e, 1, r, :].astype(SINGLE)
            kg[r, e, :] = total[:, 0:256]
            vg[r, e, :] = total[:, 256:512]
            return 0

        lax.fori_loop(0, 8, final, 0)
    writes = [
        pltpu.make_async_copy(kg, kg_any, lsem.at[0]),
        pltpu.make_async_copy(vg, vg_any, lsem.at[1]),
    ]
    for d in writes:
        d.start()
    for i in range(4):
        got(XR.at[i], xs.at[i], xr.at[i])
        tg[:, pl.ds(pl.multiple_of(matecols + 512 * i, 512), 512)] = XR[i]
    writes.append(pltpu.make_async_copy(tg, tg_any, lsem.at[2]))
    writes[2].start()
    flush()
    for d in writes:
        d.wait()
    drain_mem(QGS, qs, qr)


def place(tg, kg, vg, tg_out, kg_out, vg_out, tv, kv, vv, sems):
    parts = [(a, v, b, 128 * i) for a, v, b in ((kg, kv, kg_out), (vg, vv, vg_out)) for i in range(2)]
    parts += [(tg, tv, tg_out, 32 * i) for i in range(4)]
    ins, outs = [], []
    for n, (a, v, b, start) in enumerate(parts):
        rows = pl.ds(start, 32 if n >= 4 else 128)
        ins.append(pltpu.make_async_copy(a.at[rows], v.at[rows], sems.at[0, n]))
        outs.append(pltpu.make_async_copy(v.at[rows], b.at[rows], sems.at[1, n]))
    for d in ins:
        d.start()
    for d, o in zip(ins, outs):
        d.wait()
        o.start()
    for o in outs:
        o.wait()


def shards(tokens, picks, route_weight, cotangent, query_weight, key_weight, value_weight, gates):
    anywhere = pl.BlockSpec(memory_space=pl.ANY)
    vmem = pl.BlockSpec(memory_space=pltpu.VMEM)
    V = pltpu.VMEM
    S = pltpu.SemaphoreType.DMA
    tg, kg, vg = pl.pallas_call(
        kernel,
        out_shape=(
            jax.ShapeDtypeStruct((128, 4096), HALF),
            jax.ShapeDtypeStruct((256, 2, 256), SINGLE),
            jax.ShapeDtypeStruct((256, 2, 256), SINGLE),
        ),
        in_specs=[
            anywhere, vmem, vmem, anywhere, anywhere, anywhere, anywhere,
            pl.BlockSpec(memory_space=pltpu.SMEM),
        ],
        out_specs=(anywhere, anywhere, anywhere),
        scratch_shapes=[
            V((256, 2, 256), HALF),
            V((256, 2, 256), HALF),
            V((128, 4096), HALF),
            V((256, 2, 256), SINGLE),
            V((256, 2, 256), SINGLE),
            V((8, 128, 4096), HALF),
            V((8, 128, 512), HALF),
            V((8, 8, 128), SINGLE),
            V((2, 16, 256, 512), HALF),
            V((4096, 256), HALF),
            V((2, 4, 48, 4096), HALF),
            V((4, 128, 256), HALF),
            V((2, 4, 48, 256), HALF),
            V((2, 4, 4, 48, 1024), HALF),
            V((2, 4, 192, 512), HALF),
            V((2, 3, 256, 512), HALF),
            V((2, 2, 128, 512), HALF),
            V((2, 2, 256, 512), HALF),
            V((2, 256, 512), SINGLE),
            V((2, 4, 96, 2048), HALF),
            V((8, 96, 2048), HALF),
            V((4, 128, 512), HALF),
            V((4, 128, 512), HALF),
            V((256, 768), HALF),
            V((4, 96, 256), HALF),
            V((8, 96, 256), HALF),
            V((256, 2048), SINGLE),
            V((2, 192, 512), SINGLE),
            V((16, 8, 256), SINGLE),
        ]
        + [V((16, 32, 256), HALF)] * 8
        + [
            V((2, 4, 48, 256), HALF),
            V((2, 192, 512), HALF),
            S((5,)),
            S((2, 20)), S((2, 20)),
            S((11,)), S((11,)),
            S((11,)), S((11,)),
            S((8,)), S((8,)),
            S((16,)), S((16,)),
            S((16,)), S((16,)),
            S((16,)), S((16,)),
            S((16,)), S((16,)),
            S((16,)), S((16,)),
            S((2, 8)), S((2, 8)),
            S((2, 4)), S((2, 4)),
            S((2, 8)), S((2, 8)),
            S((8,)), S((8,)),
            S((4,)), S((4,)),
        ],
        compiler_params=pltpu.CompilerParams(
            collective_id=0, has_side_effects=True, vmem_limit_bytes=60 * 1024 * 1024
        ),
    )(
        tokens, picks.T, route_weight.T, cotangent, query_weight, key_weight, value_weight,
        gates.transpose(0, 2, 1).reshape(2, 3),
    )
    outs = (tg, kg, vg)
    return pl.pallas_call(
        place,
        out_shape=tuple(jax.ShapeDtypeStruct(o.shape, o.dtype) for o in outs),
        in_specs=[anywhere] * 3,
        out_specs=(anywhere,) * 3,
        scratch_shapes=[V(o.shape, o.dtype) for o in outs] + [S((2, 8))],
    )(*outs)


def solution(mesh):
    return jax.shard_map(
        shards,
        mesh=mesh,
        in_specs=(
            P(("ctx", "mem"), None),
            P(("ctx", "mem"), None),
            P(("ctx", "mem"), None),
            P(("ctx", "mem"), None),
            P(),
            P("ctx", "mem", None),
            P("ctx", "mem", None),
            P("ctx", None, "mem"),
        ),
        out_specs=(P(("ctx", "mem"), None), P("ctx", "mem", None), P("ctx", "mem", None)),
        check_vma=False,
    )
```

```python
import jax
import jax.numpy as jnp
from jax import lax
from jax.experimental import pallas as pl
from jax.experimental.pallas import tpu as pltpu
from jax.sharding import PartitionSpec as P

MESH = pl.DeviceIdType.MESH
HALF = jnp.bfloat16
SINGLE = jnp.float32
TN = (((0,), (0,)), ((), ()))
NT = (((1,), (1,)), ((), ()))
NN = (((1,), (0,)), ((), ()))
OFFS_OUT = (0, 3, 1, 2)
OFFS_IN = (2, 1, 3, 0)


def dot(a, b, dims):
    return lax.dot_general(a, b, dims, preferred_element_type=SINGLE)


def kernel(
    tok, picks, weight, cot, qw, kw_any, vw_any, gates,
    tg_any, kg_any, vg_any,
    kw, vw, tg, kg, vg,
    T, SIDE, MT, W, QW, OWN, SELT, QS, OS, GRS, G, F2, R2, ACC, CS, RB, XS, XR, PT, QGS, QGR, BASE, KVA,
    GB, SD, RD, SS, RSS, SW, RW, SM, RM, WT, KV,
    lsem, ws, wr, zs, zr, es, er, hs, hr, gas, gar, ds, dr, ss, sr, vs, vr, ms, mr, os_, or_, gs, gr, bs, br, qs, qr, xs, xr,
):
    c = lax.axis_index("ctx")
    m = lax.axis_index("mem")
    y, x = c // 4, c % 4
    z, k = m // 2, m % 2
    mate = m + 1 - 2 * k

    def mm(o, core):
        return ((z + o) % 4) * 2 + core

    pos = ((x, y), (y, x))

    def idx(e, p, s):
        return (s % 4) * 4 + p % 4 if e == 0 else (p % 4) * 4 + s % 4

    def to(e, dp, dsec):
        p, s = pos[e]
        return (idx(e, p + dp, s + dsec), m)

    def rc(src, dst, ssem, rsem, dev):
        return pltpu.make_async_remote_copy(
            src_ref=src, dst_ref=dst, send_sem=ssem, recv_sem=rsem,
            device_id=dev, device_id_type=MESH,
        )

    pending = []

    def send(src, dst, ssem, rsem, dev):
        d = rc(src, dst, ssem, rsem, dev)
        d.start()
        pending.append(d)

    def flush():
        for d in pending:
            d.wait_send()
        pending.clear()

    def got(ref, ssem, rsem):
        rc(ref, ref, ssem, rsem, (c, mate)).wait_recv()

    weights_ = [
        pltpu.make_async_copy(kw_any, kw, lsem.at[3]),
        pltpu.make_async_copy(vw_any, vw, lsem.at[4]),
    ]
    for d in weights_:
        d.start()
    locals_ = [
        pltpu.make_async_copy(tok, T.at[m], lsem.at[0]),
        pltpu.make_async_copy(qw, QW, lsem.at[1]),
        pltpu.make_async_copy(cot, SIDE.at[m, :, pl.ds(0, 256)], lsem.at[2]),
    ]
    for d in locals_:
        d.start()

    barrier = pltpu.get_barrier_semaphore()

    def greet(off, _):
        pl.semaphore_signal(barrier, inc=1, device_id=((c + off) % 16, m), device_id_type=MESH)
        return 0

    def greet_mem(off, _):
        pl.semaphore_signal(barrier, inc=1, device_id=(c, (m + off) % 8), device_id_type=MESH)
        return 0

    lax.fori_loop(1, 16, greet, 0)
    lax.fori_loop(1, 8, greet_mem, 0)
    for d in weights_:
        d.wait()
    for e in range(2):
        W[e, c, :, 0:256] = kw[:, e, :]
        W[e, c, :, 256:512] = vw[:, e, :]
        for g in range(3):
            GB[c, 2 * g + e:2 * g + e + 1, :] = jnp.full((1, 256), gates[e, g], SINGLE)
    GB[c, 6:8, :] = jnp.zeros((2, 256), SINGLE)
    MT[m] = jnp.concatenate(
        [picks[...].astype(SINGLE), weight[...].astype(SINGLE), jnp.zeros((4, 128), SINGLE)], axis=0
    )
    pl.semaphore_wait(barrier, 22)

    TOP, BOT = pl.ds(0, 64), pl.ds(64, 64)
    up, down, part = (c, mm(1, k)), (c, mm(3, k)), (c, mate)

    def zsend(buf, sems, slot, rows, n, dev):
        r = buf.at[slot] if rows is None else buf.at[slot, rows]
        send(r, r, sems[0].at[n], sems[1].at[n], dev)

    def zgot(buf, sems, slot, rows, n):
        got(buf.at[slot] if rows is None else buf.at[slot, rows], sems[0].at[n], sems[1].at[n])

    tz, ez = (zs, zr), (es, er)

    def z_start(buf, sems):
        zsend(buf, sems, m, TOP, 0, up)
        zsend(buf, sems, m, BOT, 1, down)
        zsend(buf, sems, m, BOT, 2, up)
        zsend(buf, sems, m, TOP, 3, down)
        zsend(buf, sems, m, None, 6, part)

    def z_forward(buf, sems):
        zgot(buf, sems, mm(3, k), TOP, 0)
        zsend(buf, sems, mm(3, k), TOP, 4, up)
        zgot(buf, sems, mm(1, k), BOT, 1)
        zsend(buf, sems, mm(1, k), BOT, 5, down)

    def z_hand(buf, sems):
        zgot(buf, sems, mm(3, k), BOT, 2)
        zsend(buf, sems, mm(3, k), None, 7, part)
        zgot(buf, sems, mm(1, k), TOP, 3)
        zsend(buf, sems, mm(1, k), None, 8, part)

    def z_far(buf, sems):
        zgot(buf, sems, mm(2, k), TOP, 4)
        zsend(buf, sems, mm(2, k), TOP, 9, part)
        zgot(buf, sems, mm(2, k), BOT, 5)
        zsend(buf, sems, mm(2, k), BOT, 10, part)

    def z_mate(buf, sems, o):
        if o == 2:
            zgot(buf, sems, mm(2, 1 - k), TOP, 9)
            zgot(buf, sems, mm(2, 1 - k), BOT, 10)
        else:
            zgot(buf, sems, mm(o, 1 - k), None, {0: 6, 3: 7, 1: 8}[o])

    HT, HB = pl.ds(0, 128), pl.ds(128, 128)

    def wsend(e, block, rows, n, dp, dsec):
        r = W.at[e, block] if rows is None else W.at[e, block, rows]
        send(r, r, ws.at[e, n], wr.at[e, n], to(e, dp, dsec))

    def wgot(e, block, rows, n):
        got(W.at[e, block] if rows is None else W.at[e, block, rows], ws.at[e, n], wr.at[e, n])

    def send_gate(off, _):
        there = (c + off) % 16
        rc(GB.at[c], GB.at[c], gas.at[off], gar.at[off], (there, m)).start()
        return 0

    def send_meta(off, _):
        there = (m + off) % 8
        rc(MT.at[m], MT.at[m], hs.at[off], hr.at[off], (c, there)).start()
        return 0

    for e in range(2):
        wsend(e, c, None, 0, 1, 0)
        wsend(e, c, None, 1, 3, 0)
    for e in range(2):
        wsend(e, c, None, 4, 0, 1)
        wsend(e, c, None, 5, 0, 3)
    lax.fori_loop(1, 8, send_meta, 0)
    for d in locals_:
        d.wait()
    SIDE[m, :, 256:512] = dot(T[m], QW[...], NN).astype(HALF)
    zsend(SIDE, ez, m, None, 2, (c, mm(2, k)))
    zsend(SIDE, ez, m, None, 0, up)
    zsend(SIDE, ez, m, None, 1, down)
    zsend(SIDE, ez, m, None, 6, part)
    z_start(T, tz)
    lax.fori_loop(1, 16, send_gate, 0)

    def side_hand(o):
        n = {3: 0, 1: 1, 2: 2}[o]
        zgot(SIDE, ez, mm(o, k), None, n)
        zsend(SIDE, ez, mm(o, k), None, 7 + n, part)

    def side_mate(o):
        zgot(SIDE, ez, mm(o, 1 - k), None, {0: 6, 3: 7, 1: 8, 2: 9}[o])

    def w_first(e):
        p, s = pos[e]
        b = idx(e, p + 3, s)
        wgot(e, b, None, 0)
        wsend(e, b, HT, 2, 1, 0)
        b = idx(e, p + 1, s)
        wgot(e, b, None, 1)
        wsend(e, b, HB, 3, 3, 0)

    def w_spread(e, i):
        p, s = pos[e]
        b = idx(e, p + OFFS_OUT[i], s)
        wsend(e, b, None, 4 + 4 * i, 0, 1)
        wsend(e, b, None, 5 + 4 * i, 0, 3)

    def w_far(e):
        p, s = pos[e]
        b = idx(e, p + 2, s)
        wgot(e, b, HT, 2)
        wgot(e, b, HB, 3)

    def w_second(e, i):
        p, s = pos[e]
        b = idx(e, p + OFFS_OUT[i], s + 3)
        wgot(e, b, None, 4 + 4 * i)
        wsend(e, b, HT, 6 + 4 * i, 0, 1)
        b = idx(e, p + OFFS_OUT[i], s + 1)
        wgot(e, b, None, 5 + 4 * i)
        wsend(e, b, HB, 7 + 4 * i, 0, 3)

    def w_last(e, i):
        p, s = pos[e]
        b = idx(e, p + OFFS_OUT[i], s + 2)
        wgot(e, b, HT, 6 + 4 * i)
        wgot(e, b, HB, 7 + 4 * i)

    sub = lax.broadcasted_iota(jnp.int32, (128, 128), 0)
    lane = lax.broadcasted_iota(jnp.int32, (128, 128), 1)
    before = jnp.where(sub < lane, 1.0, 0.0).astype(HALF)
    subf = sub.astype(SINGLE)
    mf = m.astype(SINGLE)

    def positions(d, core):
        meta = MT[d]
        p0, p1 = meta[0:1], meta[1:2]
        hits = jnp.where((subf == p0) | (subf == p1), 1.0, 0.0).astype(HALF)
        rank = dot(hits, before, NN)
        out = []
        for pk in (p0, p1):
            r = jnp.sum(jnp.where(subf == pk, rank, 0.0), axis=0, keepdims=True)
            out.append(48.0 * pk + 24.0 * core + r)
        return out

    def gather_side(o):
        zz = (z + o) % 4
        ws_, sels = [], []
        for core in range(2):
            p0, p1 = positions(2 * zz + core, float(core))
            at = subf + 96.0 * mf
            sel = jnp.where(((at == p0) | (at == p1)) & (sub < 96), 1.0, 0.0)
            meta = MT[2 * zz + core]
            w = []
            for e in range(2):
                pick = jnp.where(meta[0:1] == 2.0 * mf + e, meta[2:3], meta[3:4])
                w.append(jnp.sum(sel[48 * e:48 * e + 48] * pick, axis=1, keepdims=True))
            ws_.append(w)
            sels.append(sel.astype(HALF))
        sel = jnp.concatenate(sels, axis=1)
        SELT[zz] = sel
        got_side = dot(sel, SIDE[pl.ds(2 * zz, 2)].reshape(256, 512), NN)
        for e in range(2):
            w = ws_[0][e] + ws_[1][e]
            rows = got_side[48 * e:48 * e + 48]
            WT[e, zz] = (w * rows[:, 0:256]).astype(HALF)
            QS[e, zz] = rows[:, 256:512].astype(HALF)

    def gather(o):
        zz = (z + o) % 4
        for a in range(0, 4096, 1024):
            picked = dot(SELT[zz], T[pl.ds(2 * zz, 2), :, a:a + 1024].reshape(256, 1024), NN).astype(HALF)
            OWN[0, zz, :, a:a + 1024] = picked[0:48]
            for j in range(4):
                q = 1024 * j + a // 4
                OWN[1, zz, :, q:q + 256] = picked[48:96, 256 * j:256 * j + 256]

    def exchange(src, dst, ssem, rsem):
        def one(off, _):
            there = (c + off) % 16
            rc(src.at[there], dst.at[c], ssem.at[off], rsem.at[off], (there, m)).start()
            return 0

        lax.fori_loop(1, 16, one, 0)
        dst[c] = src[c]

    def collect(dst, ssem, rsem):
        def one(off, _):
            rc(dst.at[0], dst.at[(c - off + 16) % 16], ssem.at[off], rsem.at[off], (c, mate)).wait_recv()
            return 0

        lax.fori_loop(1, 16, one, 0)

    def drain(src, ssem, rsem):
        def one(off, _):
            rc(src.at[0], src.at[0], ssem.at[off], rsem.at[off], (c, mate)).wait_send()
            return 0

        lax.fori_loop(1, 16, one, 0)

    def collect_mem(dst, ssem, rsem):
        def one(off, _):
            rc(dst.at[0], dst.at[(m - off + 8) % 8], ssem.at[off], rsem.at[off], (c, mate)).wait_recv()
            return 0

        lax.fori_loop(1, 8, one, 0)

    def drain_mem(src, ssem, rsem):
        def one(off, _):
            rc(src.at[0], src.at[0], ssem.at[off], rsem.at[off], (c, mate)).wait_send()
            return 0

        lax.fori_loop(1, 8, one, 0)

    def gate(at, which):
        g = GB[at]
        return jnp.concatenate(
            [jnp.broadcast_to(g[2 * which + e:2 * which + e + 1], (16, 256)) for e in range(2)], axis=0
        )

    def kv_part(e, i):
        p, s = pos[e]
        total = KVA[e] if i else jnp.zeros((192, 512), SINGLE)
        for o in range(4):
            b = idx(e, p + OFFS_OUT[i], s + o)
            q = (s + o) % 4 * 4 + (p + OFFS_OUT[i]) % 4
            cols = OWN[e, :, :, pl.ds(pl.multiple_of(q * 256, 256), 256)].reshape(192, 256)
            total = total + dot(cols, W[e, b], NN)
        if i < 3:
            KVA[e] = total
        else:
            KV[e] = total.astype(HALF)

    def back(i, carry):
        at = 15 - i
        ct, ca = carry
        total = RD[at].astype(SINGLE) + ct
        adj = total + ca
        SS[at] = (gate(at, 2) * adj).astype(HALF)
        return gate(at, 1) * total, gate(at, 0) * adj

    zero = jnp.zeros((32, 256), SINGLE)
    w_first(0)
    w_first(1)
    w_spread(0, 1)
    w_spread(1, 1)
    for o in (3, 1, 2):
        side_hand(o)
    collect_mem(MT, hs, hr)
    for o in (0, 3, 1, 2):
        side_mate(o)
        gather_side(o)
    for e in range(2):
        direct = dot(WT[e].reshape(192, 256), QS[e].reshape(192, 256), TN).astype(HALF)
        SD[:, 16 * e:16 * e + 16, :] = direct.reshape(16, 16, 256)
    exchange(SD, RD, ds, dr)
    w_spread(0, 2)
    w_spread(1, 2)
    z_mate(T, tz, 0)
    gather(0)
    w_far(0)
    w_far(1)
    w_spread(0, 3)
    w_spread(1, 3)
    w_second(0, 0)
    w_second(1, 0)
    z_forward(T, tz)
    rows768 = lax.broadcasted_iota(jnp.int32, (768, 128), 0).astype(SINGLE)
    kf = k.astype(SINGLE)
    for half, (d, core) in enumerate(((m, kf), (mate, 1.0 - kf))):
        p0, p1 = positions(d, core)
        hot = jnp.where((rows768 == p0) | (rows768 == p1), 1.0, 0.0)
        PT[128 * half:128 * half + 128, :] = hot.T.astype(HALF)
    collect(GB, gas, gar)
    collect(RD, ds, dr)
    lax.fori_loop(0, 16, back, (zero, zero))
    exchange(SS, RSS, ss, sr)
    w_second(0, 1)
    w_second(1, 1)
    w_second(0, 2)
    w_second(1, 2)
    z_hand(T, tz)
    z_mate(T, tz, 3)
    gather(3)
    w_second(0, 3)
    w_second(1, 3)
    z_mate(T, tz, 1)
    gather(1)
    collect(RSS, ss, sr)
    z_far(T, tz)
    z_mate(T, tz, 2)
    gather(2)

    early = list(pending)
    pending.clear()

    def slices(e, o):
        p, s = pos[e]
        cols = pl.ds(pl.multiple_of((s + o) % 4 * 1024, 1024), 1024)
        send(OWN.at[e, :, :, cols], OS.at[e, s], os_.at[e, o], or_.at[e, o], to(e, 0, o))

    keep = []
    for e in range(2):
        slices(e, 2)
        s = pos[e][1]
        own = OWN.at[e, :, :, pl.ds(pl.multiple_of(s * 1024, 1024), 1024)]
        keep.append(pltpu.make_async_copy(own, OS.at[e, s], lsem.at[e]))
        keep[e].start()

    for i in range(4):
        for e in range(2):
            w_last(e, i)
            kv_part(e, i)
    for e in range(2):
        written = dot(KV[e, :, 256:512], KV[e, :, 0:256], TN)
        written = GB[c, 4 + e:5 + e, :] * written
        SW[:, 16 * e:16 * e + 16, :] = written.astype(HALF).reshape(16, 16, 256)
    exchange(SW, RW, vs, vr)
    for e in range(2):
        scaled = RSS[:, 16 * e:16 * e + 16, :].reshape(256, 256)
        s = pos[e][1]
        GRS[e, s, :, 0:256] = dot(KV[e, :, 256:512], scaled, NN).astype(HALF)
        GRS[e, s, :, 256:512] = dot(KV[e, :, 0:256], scaled, NT).astype(HALF)
        for o in (1, 3):
            send(GRS.at[e, s], GRS.at[e, s], os_.at[e, 4 + o], or_.at[e, 4 + o], to(e, 0, o))

    def gsend(src, dst, e, n, dp):
        send(src, dst, gs.at[e, n], gr.at[e, n], to(e, dp, 0))

    def s_forward(e):
        s = pos[e][1]
        before_, after = (s + 3) % 4, (s + 1) % 4
        got(GRS.at[e, before_], os_.at[e, 5], or_.at[e, 5])
        ref = GRS.at[e, before_, pl.ds(0, 96)]
        send(ref, ref, os_.at[e, 6], or_.at[e, 6], to(e, 0, 1))
        got(GRS.at[e, after], os_.at[e, 7], or_.at[e, 7])
        ref = GRS.at[e, after, pl.ds(96, 96)]
        send(ref, ref, os_.at[e, 4], or_.at[e, 4], to(e, 0, 3))

    def s_wait(e):
        s = pos[e][1]
        keep[e].wait()
        got(GRS.at[e, (s + 2) % 4, pl.ds(0, 96)], os_.at[e, 6], or_.at[e, 6])
        got(GRS.at[e, (s + 2) % 4, pl.ds(96, 96)], os_.at[e, 4], or_.at[e, 4])
        for o in (2, 1, 3):
            got(OS.at[e, (s - o + 4) % 4], os_.at[e, o], or_.at[e, o])

    def share(e, i):
        block = (pos[e][0] + OFFS_IN[i]) % 4
        cols = OS[e, :, :, :, pl.ds(pl.multiple_of(block * 256, 256), 256)].reshape(768, 256)
        total = dot(cols, GRS[e].reshape(768, 512), TN)
        if i == 3:
            ACC[e] = total
        else:
            G[e, i] = total.astype(HALF)
        if i == 0:
            gsend(G.at[e, 0, HT], F2.at[e, 0], e, 0, 1)
            gsend(G.at[e, 0, HB], F2.at[e, 1], e, 1, 3)

    def forth(at, carry):
        state, memory = carry
        state = gate(at, 0) * state + RW[at].astype(SINGLE)
        memory = gate(at, 1) * memory + state
        SM[at] = memory.astype(HALF)
        return state, memory

    def add_rows(dst, parts, start, rows, out=None):
        def one(i, _):
            r = pl.ds(pl.multiple_of(start + i * 32, 32), 32)
            total = dst[r, :].astype(SINGLE)
            for ref, base in parts:
                total = total + ref[pl.ds(pl.multiple_of(base + i * 32, 32), 32), :].astype(SINGLE)
            if out is None:
                dst[r, :] = total.astype(HALF)
            else:
                out[r, :] = total
            return 0

        lax.fori_loop(0, rows // 32, one, 0)

    def r_pass(e, i):
        got(F2.at[e, i - 1], gs.at[e, i - 1], gr.at[e, i - 1])
        add_rows(G.at[e, i], [(F2.at[e, i - 1], 0)], 128 * (i - 1), 128)
        gsend(G.at[e, i], R2.at[e, i - 1], e, 1 + i, 1 if i == 1 else 3)

    def bsend(src, dst, n, part_, slot, dev):
        send(src, dst, bs.at[part_, n], br.at[part_, slot], (c, dev))

    def contribute(h, half):
        def column(i, _):
            for e in range(2):
                out = dot(GRS[e, pos[e][1]], W[e, 8 * h + i], NT)
                CS[h, :, 48 * e:48 * e + 48, pl.ds(pl.multiple_of(i * 256, 256), 256)] = (
                    out.astype(HALF).reshape(4, 48, 256)
                )
            return 0

        lax.fori_loop(4 * half, 4 * half + 4, column, 0)

    def dispatch(h, half, chips):
        cols = pl.ds(1024 * half, 1024)
        for o in chips:
            bsend(CS.at[h, (z + o) % 4, :, cols], RB.at[m, :, cols], 4 * h + o, half, m, mm(o, h))

    contribute(0, 0)
    dispatch(0, 0, (2, 1, 3))
    contribute(0, 1)
    dispatch(0, 1, (2, 1, 3))
    for e in range(2):
        slices(e, 1)
    collect(RW, vs, vr)
    lax.fori_loop(0, 16, forth, (zero, zero))
    exchange(SM, RM, ms, mr)
    for e in range(2):
        slices(e, 3)
    contribute(1, 0)
    dispatch(1, 0, (2, 1, 3))
    s_forward(0)
    s_forward(1)
    contribute(1, 1)
    dispatch(1, 1, (2,))

    collect(RM, ms, mr)
    for e in range(2):
        memory = RM[:, 16 * e:16 * e + 16, :].reshape(256, 256)
        grad = dot(WT[e].reshape(192, 256), memory, NN).astype(HALF)
        QGS[:, 48 * e:48 * e + 48, :] = grad.reshape(4, 48, 256)

    def send_query(off, _):
        there = (m + off) % 8
        rc(QGS.at[there // 2], QGR.at[m], qs.at[off], qr.at[off], (c, there)).start()
        return 0

    lax.fori_loop(1, 8, send_query, 0)
    QGR[m] = QGS[z]
    dispatch(1, 1, (1, 3))
    for half in range(2):
        cols = pl.ds(1024 * half, 1024)
        bsend(CS.at[1 - k, z, :, cols], RB.at[m, :, cols], 0, half, m, mate)
    RB[m] = CS[k, z]
    for e in range(2):
        s_wait(e)
        share(e, 0)
    for i in (1, 2, 3):
        for e in range(2):
            share(e, i)
    for i in (1, 2):
        for e in range(2):
            r_pass(e, i)
    for d in early:
        d.wait_send()
    drain(GB, gas, gar)
    drain(SD, ds, dr)
    drain(SS, ss, sr)
    drain(SW, vs, vr)
    drain(SM, ms, mr)
    drain_mem(MT, hs, hr)
    collect_mem(QGR, qs, qr)
    grads = dot(PT[...], QGR[...].reshape(768, 256), NN).astype(HALF)

    def base(i, _):
        n = pl.multiple_of(i * 512, 512)
        BASE[:, pl.ds(n, 512)] = dot(grads, QW[pl.ds(pl.multiple_of(k * 2048 + n, 512), 512), :], NT)
        return 0

    lax.fori_loop(0, 4, base, 0)

    mycols = pl.multiple_of(k * 2048, 2048)
    matecols = pl.multiple_of((1 - k) * 2048, 2048)
    writes = []
    for half in range(2):
        def arrived(off, _):
            there = (m + off) % 8
            cols = pl.ds(1024 * half, 1024)
            rc(RB.at[0, :, cols], RB.at[there, :, cols], bs.at[half, 0], br.at[half, there], (c, mate)).wait_recv()
            return 0

        lax.fori_loop(1, 8, arrived, 0)
        for i in (2 * half, 2 * half + 1):
            n = slice(512 * i, 512 * i + 512)
            total = (dot(PT[...], RB[:, :, n].reshape(768, 512), NN) + BASE[:, n]).astype(HALF)
            XS[i] = total[128:256]
            send(XS.at[i], XR.at[i], xs.at[i], xr.at[i], part)
            cols = pl.ds(pl.multiple_of(mycols + 512 * i, 512), 512)
            tg[i] = total[0:128]
            writes.append(pltpu.make_async_copy(tg.at[i], tg_any.at[:, cols], lsem.at[5 + i]))
            writes[-1].start()

    for e in range(2):
        got(R2.at[e, 0], gs.at[e, 2], gr.at[e, 2])
        got(R2.at[e, 1], gs.at[e, 3], gr.at[e, 3])

        def final(i, _, e=e):
            r = pl.ds(pl.multiple_of(i * 32, 32), 32)
            total = ACC[e, r, :] + R2[e, 0, r, :].astype(SINGLE) + R2[e, 1, r, :].astype(SINGLE)
            kg[r, e, :] = total[:, 0:256]
            vg[r, e, :] = total[:, 256:512]
            return 0

        lax.fori_loop(0, 8, final, 0)
    last = [
        pltpu.make_async_copy(kg, kg_any, lsem.at[0]),
        pltpu.make_async_copy(vg, vg_any, lsem.at[1]),
    ]
    for d in last:
        d.start()
    for i in range(4):
        got(XR.at[i], xs.at[i], xr.at[i])
        cols = pl.ds(pl.multiple_of(matecols + 512 * i, 512), 512)
        last.append(pltpu.make_async_copy(XR.at[i], tg_any.at[:, cols], lsem.at[9 + i]))
        last[-1].start()

    flush()
    for d in writes + last:
        d.wait()
    drain_mem(QGS, qs, qr)


def place(tg, kg, vg, tg_out, kg_out, vg_out, tv, kv, vv, sems):
    parts = [(a, v, b, 128 * i) for a, v, b in ((kg, kv, kg_out), (vg, vv, vg_out)) for i in range(2)]
    parts += [(tg, tv, tg_out, 32 * i) for i in range(4)]
    ins, outs = [], []
    for n, (a, v, b, start) in enumerate(parts):
        rows = pl.ds(start, 32 if n >= 4 else 128)
        ins.append(pltpu.make_async_copy(a.at[rows], v.at[rows], sems.at[0, n]))
        outs.append(pltpu.make_async_copy(v.at[rows], b.at[rows], sems.at[1, n]))
    for d in ins:
        d.start()
    for d, o in zip(ins, outs):
        d.wait()
        o.start()
    for o in outs:
        o.wait()


def shards(tokens, picks, route_weight, cotangent, query_weight, key_weight, value_weight, gates):
    anywhere = pl.BlockSpec(memory_space=pl.ANY)
    vmem = pl.BlockSpec(memory_space=pltpu.VMEM)
    V = pltpu.VMEM
    S = pltpu.SemaphoreType.DMA
    tg, kg, vg = pl.pallas_call(
        kernel,
        out_shape=(
            jax.ShapeDtypeStruct((128, 4096), HALF),
            jax.ShapeDtypeStruct((256, 2, 256), SINGLE),
            jax.ShapeDtypeStruct((256, 2, 256), SINGLE),
        ),
        in_specs=[
            anywhere, vmem, vmem, anywhere, anywhere, anywhere, anywhere,
            pl.BlockSpec(memory_space=pltpu.SMEM),
        ],
        out_specs=(anywhere, anywhere, anywhere),
        scratch_shapes=[
            V((256, 2, 256), HALF),
            V((256, 2, 256), HALF),
            V((4, 128, 512), HALF),
            V((256, 2, 256), SINGLE),
            V((256, 2, 256), SINGLE),
            V((8, 128, 4096), HALF),
            V((8, 128, 512), HALF),
            V((8, 8, 128), SINGLE),
            V((2, 16, 256, 512), HALF),
            V((4096, 256), HALF),
            V((2, 4, 48, 4096), HALF),
            V((4, 128, 256), HALF),
            V((2, 4, 48, 256), HALF),
            V((2, 4, 4, 48, 1024), HALF),
            V((2, 4, 192, 512), HALF),
            V((2, 3, 256, 512), HALF),
            V((2, 2, 128, 512), HALF),
            V((2, 2, 256, 512), HALF),
            V((2, 256, 512), SINGLE),
            V((2, 4, 96, 2048), HALF),
            V((8, 96, 2048), HALF),
            V((4, 128, 512), HALF),
            V((4, 128, 512), HALF),
            V((256, 768), HALF),
            V((4, 96, 256), HALF),
            V((8, 96, 256), HALF),
            V((256, 2048), SINGLE),
            V((2, 192, 512), SINGLE),
            V((16, 8, 256), SINGLE),
        ]
        + [V((16, 32, 256), HALF)] * 8
        + [
            V((2, 4, 48, 256), HALF),
            V((2, 192, 512), HALF),
            S((13,)),
            S((2, 20)), S((2, 20)),
            S((11,)), S((11,)),
            S((11,)), S((11,)),
            S((8,)), S((8,)),
            S((16,)), S((16,)),
            S((16,)), S((16,)),
            S((16,)), S((16,)),
            S((16,)), S((16,)),
            S((16,)), S((16,)),
            S((2, 8)), S((2, 8)),
            S((2, 4)), S((2, 4)),
            S((2, 8)), S((2, 8)),
            S((8,)), S((8,)),
            S((4,)), S((4,)),
        ],
        compiler_params=pltpu.CompilerParams(
            collective_id=0, has_side_effects=True, vmem_limit_bytes=60 * 1024 * 1024
        ),
    )(
        tokens, picks.T, route_weight.T, cotangent, query_weight, key_weight, value_weight,
        gates.transpose(0, 2, 1).reshape(2, 3),
    )
    outs = (tg, kg, vg)
    return pl.pallas_call(
        place,
        out_shape=tuple(jax.ShapeDtypeStruct(o.shape, o.dtype) for o in outs),
        in_specs=[anywhere] * 3,
        out_specs=(anywhere,) * 3,
        scratch_shapes=[V(o.shape, o.dtype) for o in outs] + [S((2, 8))],
    )(*outs)


def solution(mesh):
    return jax.shard_map(
        shards,
        mesh=mesh,
        in_specs=(
            P(("ctx", "mem"), None),
            P(("ctx", "mem"), None),
            P(("ctx", "mem"), None),
            P(("ctx", "mem"), None),
            P(),
            P("ctx", "mem", None),
            P("ctx", "mem", None),
            P("ctx", None, "mem"),
        ),
        out_specs=(P(("ctx", "mem"), None), P("ctx", "mem", None), P("ctx", "mem", None)),
        check_vma=False,
    )
```
